128 devices in a mesh: dev: 128 (over y, z, x, core).
Axes of the slice: x: 4, y: 4, z: 4, core: 2. Of those that a mesh axis runs over, the one named last changes fastest.
Arguments:
- h_self: bfloat16 [65536, 512], P('dev'), may hold values from -6 to 6
- agg: bfloat16 [65536, 512], P('dev'), may hold values from -6 to 6
- grad_out: bfloat16 [65536, 512], P('dev'), may hold values from -6 to 6
- w_self: bfloat16 [512, 512], replicated, may hold values from -0.25 to 0.25
- w_neigh: bfloat16 [512, 512], replicated, may hold values from -0.25 to 0.25
- owner: int32 [65536, 3, 1], P('dev'), may hold values from 0 to 127; in each aligned block of 1536 rows (0 to 1535, 1536 to 3071, ..., all dimensions but the last counted through in order) at most 18 rows name the same one
- slot: int32 [65536, 3], P('dev'), may hold values from 0 to 2047
- hub_refs: int32 [65536, 2], P('dev'), may hold values from 0 to 1023
Outputs:
- grad_self: bfloat16 [65536, 512], P('dev')
- front_grad: float32 [262144, 512], P('dev')
- hub_grad: float32 [1024, 512], replicated
- grad_w_self: float32 [512, 512], replicated
- grad_w_neigh: float32 [512, 512], replicated
The draws below stay inside these ranges and needn't reach their ends.
Inputs may be any that keep to these rules, and one draw needn't show every extreme that they name: Among the 1536 references of one device's targets (aligned blocks of rows), no owner is named more than 18 times, a bound that some block reaches.
All inputs are finite; a program needn't handle non-finite values.
Results may differ from the reference program's by a relative error of at most 0.006.
Values may be sent and summed in bfloat16 or wider, within the bound.
No kernel may reach another device: no remote copies, remote signals or barrier semaphores. Data moves between devices by JAX's collectives and lax.ppermute only.
A program may use at most 64 MiB of HBM per device.

```python
import math
import jax
import jax.numpy as jnp
import numpy as np

D = 512
H = 512
TGT_DEV = 512
OWN_DEV = 2048
HUBS = 1024
FANOUT = 5
HUB_FAN = 2
FAN = 3
CAP = 18
TARGETS = 65536
N_DEV = 128


def set_ends(entries, stream_key, least, high):
    dims = entries.shape
    index_at = [jax.random.randint(jax.random.fold_in(stream_key, axis), (), 0, dims[axis]) for axis in range(len(dims))]
    entries = entries.at[tuple(index_at)].set(least)
    longest = dims.index(max(dims))
    index_at[longest] = (index_at[longest] + 1) % dims[longest]
    return entries.at[tuple(index_at)].set(high)


def shard_levels(key, extent, shards, smallest, high):
    loudness = 1.0
    for axis_at, blocks in shards:
        draws = jax.random.uniform(jax.random.fold_in(jax.random.fold_in(key, 6), axis_at), (blocks,), jnp.float32, smallest / len(shards), high / len(shards))
        loudness = loudness * jnp.repeat(jnp.exp(draws), extent[axis_at] // blocks).reshape((-1,) + (1,) * (len(extent) - 1 - axis_at))
    return loudness


def cumulative_ranks(amount, skew):
    loads = [(1 << 20) // math.isqrt(standing ** skew) + 1 for standing in range(1, amount + 1)]
    width = 1 + sum(loads) // (1 << 30)
    return np.cumsum(np.array([max(1, weight // width) for weight in loads]))


def skewed_ids(own_key, extent, amount, lean):
    table = cumulative_ranks(amount, lean)
    lot = jax.random.randint(jax.random.fold_in(own_key, 1), extent, 0, int(table[amount - 1]))
    standing = jnp.searchsorted(jnp.asarray(table, jnp.int32), lot, side="right")
    return jax.random.permutation(jax.random.fold_in(own_key, 2), amount)[standing].astype(jnp.int32)


def deal_out(own_key, own, number, rows, amount, top, most, slope):
    order = jax.random.permutation(own_key, amount)
    heavy_load, ordinary = portions_of(amount, rows * top, most, slope, True), portions_of(amount, rows * top, most, slope, False)
    places = jnp.arange(amount)

    def named(tallies, turn):
        used = int((tallies > 0).sum())
        fixed = max(1, used // 4)
        moved = fixed + (places - fixed + turn * (used - fixed)) % max(1, amount - fixed)
        return jnp.zeros((amount,), jnp.int32).at[order[jnp.where(places < fixed, places, moved)]].set(jnp.asarray(tallies, jnp.int32))

    tallies = jnp.where(number % 4 == 0, named(heavy_load, number // 4), named(ordinary, number - number // 4 - 1))
    mixed = jax.random.permutation(jax.random.fold_in(own, 3), amount)
    source_of, taker = mixed[0:amount // 2 * 2:2], mixed[1:amount // 2 * 2:2]
    room = jnp.minimum(tallies[source_of] - 1, most - tallies[taker]) // 2
    room = jnp.where((source_of == order[0]) | (taker == order[0]) | (tallies[taker] == 0), 0, jnp.maximum(room, 0))
    moved = jax.random.randint(jax.random.fold_in(own, 4), (amount // 2,), 0, 1 << 20) % (room + 1)
    tallies = tallies.at[source_of].add(-moved).at[taker].add(moved)
    labels = jnp.searchsorted(jnp.cumsum(tallies), jnp.arange(rows * top), side="right").astype(jnp.int32)
    grid = labels.reshape(top, rows).T
    grid = grid[jax.random.permutation(jax.random.fold_in(own, 1), rows)]
    turn = jax.random.randint(jax.random.fold_in(own, 2), (rows, 1), 0, top)
    return jnp.take_along_axis(grid, (jnp.arange(top)[None, :] + turn) % top, axis=1)


def portions_of(amount, total, bound, slope, full):
    loads = [(1 << 20) // math.isqrt(standing ** slope) + 1 for standing in range(1, amount + 1)]
    largest = bound if full else min(bound, max(-(-total // amount), total * loads[0] // sum(loads)))
    least = 1 if total - largest >= amount - 1 else 0
    holding, spare = [largest] + [least] * (amount - 1), total - largest - least * (amount - 1)
    while spare > 0:
        movable = [i for i in range(1, amount) if holding[i] < largest] or [i for i in range(1, amount) if holding[i] < bound]
        mass, left = sum([loads[i] for i in movable]), spare
        for i in movable:
            more = min(bound - holding[i], max(1, left * loads[i] // mass), spare)
            holding[i] = holding[i] + more
            spare = spare - more
    return np.array(holding)


def bell_draw(key, extent, spread, limit, pieces=(), dtype=jnp.bfloat16):
    array = jax.random.normal(key, extent, jnp.float32) * spread
    if len(pieces) > 0:
        array = shard_levels(key, extent, pieces, -0.22, 0.18) * array
    return jnp.clip(array, min=-limit, max=limit).astype(dtype)


def setup_inputs(seed: int = 0) -> dict:
    key_of = jax.random.split(jax.random.key(seed), 9)
    h_self = bell_draw(key_of[0], (TARGETS, D), 1.0, 6.0, ((0, 128),))
    agg = bell_draw(key_of[1], (TARGETS, D), 1.0, 6.0, ((0, 128),))
    grad_out = bell_draw(key_of[2], (TARGETS, H), 1.0, 6.0, ((0, 128),))
    w_self = bell_draw(key_of[3], (D, H), D ** -0.5, 0.25)
    w_neigh = bell_draw(key_of[4], (D, H), D ** -0.5, 0.25)
    owner_keys = jax.random.split(jax.random.fold_in(key_of[5], 1), TARGETS * FAN // (TGT_DEV * FAN))
    owner_turns = jax.random.permutation(jax.random.fold_in(key_of[5], 3), TARGETS * FAN // (TGT_DEV * FAN))
    owner = jax.vmap(lambda own, number: deal_out(jax.random.fold_in(key_of[5], 2), own, number, TGT_DEV * FAN, N_DEV, 1, CAP, 2))(owner_keys, owner_turns).reshape((TARGETS, FAN, 1))
    slot = set_ends(jax.random.randint(key_of[6], (TARGETS, FAN), 0, OWN_DEV), jax.random.fold_in(key_of[6], 1), 0, OWN_DEV - 1).astype(jnp.int32)
    hub_refs = set_ends(skewed_ids(key_of[7], (TARGETS, HUB_FAN), HUBS, 2), jax.random.fold_in(key_of[7], 3), 0, HUBS - 1).astype(jnp.int32)
    return {"h_self": h_self, "agg": agg, "grad_out": grad_out, "w_self": w_self, "w_neigh": w_neigh, "owner": owner, "slot": slot, "hub_refs": hub_refs}


def reference(h_self, agg, grad_out, w_self, w_neigh, owner, slot, hub_refs):
    targets = h_self.shape[0]
    pre = jnp.dot(h_self, w_self, preferred_element_type=jnp.float32) + jnp.dot(agg, w_neigh, preferred_element_type=jnp.float32)
    sig = jax.nn.sigmoid(pre)
    g = (grad_out.astype(jnp.float32) * (sig * (1.0 + pre * (1.0 - sig)))).astype(jnp.bfloat16)
    scale = 1.0 / jnp.sqrt(jnp.float32(targets))
    grad_w_self = jnp.dot(h_self.T, g, preferred_element_type=jnp.float32) * scale
    grad_w_neigh = jnp.dot(agg.T, g, preferred_element_type=jnp.float32) * scale
    grad_self = jnp.dot(g, w_self.T, preferred_element_type=jnp.float32).astype(jnp.bfloat16)
    message = (jnp.dot(g, w_neigh.T, preferred_element_type=jnp.float32) / FANOUT).astype(jnp.bfloat16)
    rows32 = message.astype(jnp.float32)
    front_grad = jnp.zeros((OWN_DEV * N_DEV, D), jnp.float32)
    for column in range(FAN):
        index = owner[:, column, 0].astype(jnp.int32) * OWN_DEV + slot[:, column].astype(jnp.int32)
        front_grad = front_grad.at[index].add(rows32)
    hub_grad = jnp.zeros((HUBS, D), jnp.float32)
    for column in range(HUB_FAN):
        hub_grad = hub_grad.at[hub_refs[:, column].astype(jnp.int32)].add(rows32)
    return (grad_self, front_grad, hub_grad, grad_w_self, grad_w_neigh)
```

```python
import functools

import jax
import jax.numpy as jnp
from jax import lax
from jax.experimental import pallas as pl
from jax.experimental.pallas import tpu as pltpu
from jax.sharding import PartitionSpec as P

OWN_DEV = 2048
HUBS = 1024
FANOUT = 5
CAP = 18
MAIN = 16
REST = CAP - MAIN
FRONT = 80
CHUNK = 112
GROUP = 16
VMEM_LIMIT = 50 * 1024 * 1024
BF = jnp.bfloat16
F32 = jnp.float32
I32 = jnp.int32


def mm(a, b):
    return jnp.dot(a, b, preferred_element_type=F32)


def mm_nt(a, b):
    return lax.dot_general(a, b, (((1,), (1,)), ((), ())), preferred_element_type=F32)


def mm_tn(a, b):
    return lax.dot_general(a, b, (((0,), (0,)), ((), ())), preferred_element_type=F32)


def onehot(flag):
    return jnp.where(flag, 1.0, 0.0).astype(BF)


def grads_kernel(me, h, a, go, ws, wn, hub, grad_self, message, mine, send):
    pre = mm(h[...], ws[...]) + mm(a[...], wn[...])
    sig = jax.nn.sigmoid(pre)
    g = (go[...].astype(F32) * (sig * (1.0 + pre * (1.0 - sig)))).astype(BF)
    msg = (mm_nt(g, wn[...]) / FANOUT).astype(BF)
    message[...] = msg
    rows = lax.broadcasted_iota(I32, (HUBS, hub.shape[1]), 0)
    count = onehot(rows == hub[0:1, :]) + onehot(rows == hub[1:2, :])
    hub_part = mm(count, msg).astype(BF)
    depth = h.shape[1]
    first = lax.rem(me[0], 2) == 0
    part_self = mm_tn(h[...], g).astype(BF)
    part_neigh = mm_tn(a[...], g).astype(BF)

    @pl.when(first)
    def _():
        mine[...] = hub_part
        send[0:depth, :] = part_self
        send[depth : 2 * depth, :] = part_neigh

    @pl.when(jnp.logical_not(first))
    def _():
        send[...] = hub_part
        mine[0:depth, :] = part_self
        mine[depth : 2 * depth, :] = part_neigh

    grad_self[...] = mm_nt(g, ws[...]).astype(BF)


def spread_rows(columns):
    row = lax.broadcasted_iota(I32, (GROUP * 16, 192), 0)
    col = lax.broadcasted_iota(I32, (GROUP * 16, 192), 1)
    chunk, s = row // 16, row % 16
    want = jnp.where(s < 8, (s // 2) * 32 + chunk * 2 + s % 2, 128 + (s - 8) * 16 + chunk)
    return onehot((s < 12) & (col == want))


def pack_kernel(me, message, owner, slot, out):
    t = message.shape[0]
    n = out.shape[0]
    fan = owner.shape[0]
    device = lax.broadcasted_iota(I32, (n, t), 0)
    named = [device == owner[j : j + 1, :] for j in range(fan)]
    hot = [onehot(f) for f in named]
    before = onehot(
        lax.broadcasted_iota(I32, (t, t), 0) < lax.broadcasted_iota(I32, (t, t), 1)
    )
    base = jnp.zeros((n, 1), F32)
    ranks = []
    for j in range(fan):
        earlier = mm(hot[j], before) + base
        ranks.append(
            jnp.sum(jnp.where(named[j], earlier, 0.0), axis=0, keepdims=True).astype(I32)
        )
        base = base + jnp.sum(hot[j].astype(F32), axis=1, keepdims=True)
    pos_main = [
        jnp.where(ranks[j] < MAIN, owner[j : j + 1, :] * MAIN + ranks[j], -1) for j in range(fan)
    ]
    pos_rest = [
        jnp.where(ranks[j] >= MAIN, owner[j : j + 1, :] * REST + (ranks[j] - MAIN), -1)
        for j in range(fan)
    ]
    msg = message[...]

    lane = lax.broadcasted_iota(I32, (128, t), 0)
    at_main = (me[0] % 8) * MAIN
    at_rest = (me[0] % 64) * REST - MAIN
    kinds = [jnp.zeros((n, 128), F32) for _ in range(4)]
    for j in range(fan):
        value = slot[j : j + 1, :]
        high, low = (value // 64).astype(F32), (value % 64).astype(F32)
        in_main = ranks[j] < MAIN
        to_main = onehot(in_main & (lane == ranks[j] + at_main))
        to_rest = onehot((ranks[j] >= MAIN) & (lane == ranks[j] + at_rest))
        whole = jnp.where(named[j], 1.0, 0.0)
        a_high, a_low = (whole * high).astype(BF), (whole * low).astype(BF)
        kinds[0] = kinds[0] + mm_nt(a_high, to_main)
        kinds[1] = kinds[1] + mm_nt(a_low, to_main)
        kinds[2] = kinds[2] + mm_nt(a_high, to_rest)
        kinds[3] = kinds[3] + mm_nt(a_low, to_rest)
    kinds = [k.astype(BF) for k in kinds]

    row = lax.broadcasted_iota(I32, (GROUP * MAIN, t), 0)
    rest_row = lax.broadcasted_iota(I32, (n * REST, t), 0)
    rest_pick = (rest_row == pos_rest[0]) | (rest_row == pos_rest[1]) | (rest_row == pos_rest[2])
    rest = mm(onehot(rest_pick), msg).astype(BF)
    spread = spread_rows(192)
    for k in range(n // GROUP):
        at = row + k * GROUP * MAIN
        pick = (at == pos_main[0]) | (at == pos_main[1]) | (at == pos_main[2])
        rows = mm(onehot(pick), msg).astype(BF)
        chunks = pl.ds(k * GROUP, GROUP)
        for q in range(4):
            out[chunks, q * 16 : (q + 1) * 16, :] = rows[:, q * 128 : (q + 1) * 128].reshape(
                GROUP, 16, 128
            )
        stacked = jnp.concatenate(
            [rest[k * 32 : (k + 1) * 32, q * 128 : (q + 1) * 128] for q in range(4)]
            + [kind[k * GROUP : (k + 1) * GROUP, :] for kind in kinds],
            axis=0,
        )
        out[chunks, 64:80, :] = mm(spread, stacked).astype(BF).reshape(GROUP, 16, 128)


def join_kernel(mine, got, held, out):
    q = pl.program_id(0)
    for half in range(2):
        for step in range(2):

            @pl.when(q == step)
            def _():
                at = half * 256 + step * 128
                total = mine[:, at : at + 128].astype(F32) + got[:, at : at + 128].astype(F32)
                out[:, half, :, :] = total.astype(BF).reshape(64, 16, 128)


def reduce_kernel(received, out):
    for half in range(2):
        total = jnp.sum(received[:, half, :, :].astype(F32), axis=0).astype(BF)
        out[:, half, :, :] = jnp.broadcast_to(total[None], (64, 16, 128))


def front_kernel(received, out, rows, index):
    step = pl.program_id(0)
    n = received.shape[0]

    @pl.when(step == 0)
    def _():
        for q in range(4):
            rows[0 : n * MAIN, q * 128 : (q + 1) * 128] = received[
                :, q * 16 : (q + 1) * 16, :
            ].reshape(n * MAIN, 128)
        spread = spread_rows(192)
        main = []
        rest = [jnp.zeros((1, 128), F32), jnp.zeros((1, 128), F32)]
        for k in range(n // GROUP):
            tile = received[k * GROUP : (k + 1) * GROUP, 64:80, :].reshape(GROUP * 16, 128)
            stacked = mm_tn(spread, tile)
            for q in range(4):
                rows[n * MAIN + k * 32 : n * MAIN + (k + 1) * 32, q * 128 : (q + 1) * 128] = (
                    stacked[q * 32 : (q + 1) * 32, :].astype(BF)
                )
            main_slot = stacked[128:144, :] * 64.0 + stacked[144:160, :]
            rest_slot = stacked[160:176, :] * 64.0 + stacked[176:192, :]
            main.append(jnp.sum(main_slot[0:8, :], axis=0, keepdims=True))
            main.append(jnp.sum(main_slot[8:16, :], axis=0, keepdims=True))
            part = k * GROUP // 64
            rest[part] = rest[part] + jnp.sum(rest_slot, axis=0, keepdims=True)
        for g, line in enumerate(main + rest):
            index[g : g + 1, :] = line.astype(I32)

    block = out.shape[0]
    wanted = lax.broadcasted_iota(I32, (block, 128), 0) + step * block
    hot = jnp.concatenate(
        [onehot(wanted == index[g : g + 1, :]) for g in range(n * CAP // 128)], axis=1
    )
    out[...] = mm(hot, rows[...])


def final_kernel(scale, me, own, other, hub_grad, grad_w_self, grad_w_neigh):
    first = lax.rem(me[0], 2) == 0

    def fill(hubs, weights):
        depth = grad_w_self.shape[0]
        for half in range(2):
            for q in range(2):
                at = half * 256 + q * 128
                part = hubs[:, half, q * 16 : (q + 1) * 16, :].reshape(HUBS, 128)
                hub_grad[:, at : at + 128] = part.astype(F32)
                part = weights[:, half, q * 16 : (q + 1) * 16, :].reshape(2 * depth, 128)
                part = part.astype(F32) * scale
                grad_w_self[:, at : at + 128] = part[0:depth, :]
                grad_w_neigh[:, at : at + 128] = part[depth : 2 * depth, :]

    @pl.when(first)
    def _():
        fill(own, other)

    @pl.when(jnp.logical_not(first))
    def _():
        fill(other, own)


SMEM = pl.BlockSpec(memory_space=pltpu.SMEM)
VMEM = pl.BlockSpec(memory_space=pltpu.VMEM)
PARAMS = pltpu.CompilerParams(vmem_limit_bytes=VMEM_LIMIT)


def body(h_self, agg, grad_out, w_self, w_neigh, owner, slot, hub_refs):
    t, width = h_self.shape
    n = lax.axis_size("dev")
    me = lax.axis_index("dev").astype(I32).reshape(1)
    owner_t = owner.reshape(t, -1).T
    slot_t = slot.T
    hub_t = hub_refs.T
    swap = [(i, i ^ 1) for i in range(n)]
    half = jax.ShapeDtypeStruct((HUBS, width), BF)
    same = jax.ShapeDtypeStruct((t, width), BF)

    with jax.named_scope("grads"):
        grad_self, message, mine, send = pl.pallas_call(
            grads_kernel,
            out_shape=(same, same, half, half),
            in_specs=[SMEM] + [VMEM] * 6,
            out_specs=[VMEM] * 4,
            compiler_params=PARAMS,
        )(me, h_self, agg, grad_out, w_self, w_neigh, hub_t)
    with jax.named_scope("core_exchange"):
        got = lax.ppermute(send, "dev", swap)
    with jax.named_scope("pack"):
        packed = pl.pallas_call(
            pack_kernel,
            out_shape=jax.ShapeDtypeStruct((n, CHUNK, 128), BF),
            grid=(1,),
            in_specs=[SMEM] + [VMEM] * 3,
            out_specs=pl.BlockSpec((n, FRONT, 128), lambda i: (0, 0, 0)),
            compiler_params=PARAMS,
        )(me, message, owner_t, slot_t)
    with jax.named_scope("join"):
        packed = pl.pallas_call(
            join_kernel,
            out_shape=jax.ShapeDtypeStruct((n // 2, 2, CHUNK, 128), BF),
            grid=(2,),
            in_specs=[
                pl.BlockSpec((HUBS, width), lambda i: (0, 0)),
                pl.BlockSpec((HUBS, width), lambda i: (0, 0)),
                pl.BlockSpec(memory_space=pl.ANY),
            ],
            out_specs=pl.BlockSpec((n // 2, 2, 16, 128), lambda i: (0, 0, FRONT // 16 + i, 0)),
            input_output_aliases={2: 0},
            compiler_params=PARAMS,
        )(mine, got, packed.reshape(n // 2, 2, CHUNK, 128))
    with jax.named_scope("rows_to_owners"):
        received = lax.all_to_all(
            packed.reshape(n, CHUNK, 128), "dev", split_axis=0, concat_axis=0, tiled=True
        )
    with jax.named_scope("sum_parts"):
        total = pl.pallas_call(
            reduce_kernel,
            out_shape=jax.ShapeDtypeStruct((n // 2, 2, 32, 128), BF),
            grid=(2,),
            in_specs=[
                pl.BlockSpec((n // 2, 2, 16, 128), lambda i: (0, 0, FRONT // 16 + i, 0))
            ],
            out_specs=pl.BlockSpec((n // 2, 2, 16, 128), lambda i: (0, 0, i, 0)),
            compiler_params=PARAMS,
        )(received.reshape(n // 2, 2, CHUNK, 128))
    with jax.named_scope("sums_to_all"):
        own = lax.all_to_all(
            total.reshape(n, 32, 128), "dev", split_axis=0, concat_axis=0, tiled=True
        )
    with jax.named_scope("front"):
        front_grad = pl.pallas_call(
            front_kernel,
            out_shape=jax.ShapeDtypeStruct((OWN_DEV, width), F32),
            grid=(8,),
            in_specs=[pl.BlockSpec((n, FRONT, 128), lambda i: (0, 0, 0))],
            out_specs=pl.BlockSpec((OWN_DEV // 8, width), lambda i: (i, 0)),
            scratch_shapes=[
                pltpu.VMEM((n * CAP, width), BF),
                pltpu.VMEM((24, 128), I32),
            ],
            compiler_params=PARAMS,
            cost_estimate=pl.CostEstimate(
                flops=2 * OWN_DEV * n * CAP * width, bytes_accessed=8 << 20, transcendentals=0
            ),
        )(received)
    with jax.named_scope("core_exchange_back"):
        other = lax.ppermute(own, "dev", swap)
    scale = 1.0 / (t * n) ** 0.5
    with jax.named_scope("final"):
        hub_grad, grad_w_self, grad_w_neigh = pl.pallas_call(
            functools.partial(final_kernel, scale),
            out_shape=(
                jax.ShapeDtypeStruct((HUBS, width), F32),
                jax.ShapeDtypeStruct((width, width), F32),
                jax.ShapeDtypeStruct((width, width), F32),
            ),
            in_specs=[SMEM, VMEM, VMEM],
            out_specs=[VMEM] * 3,
            compiler_params=PARAMS,
        )(me, own.reshape(n // 2, 2, 32, 128), other.reshape(n // 2, 2, 32, 128))
    return grad_self, front_grad, hub_grad, grad_w_self, grad_w_neigh


def solution(mesh):
    placed = (
        P("dev", None),
        P("dev", None),
        P("dev", None),
        P(),
        P(),
        P("dev", None, None),
        P("dev", None),
        P("dev", None),
    )
    return jax.shard_map(
        body,
        mesh=mesh,
        in_specs=placed,
        out_specs=(P("dev", None), P("dev", None), P(), P(), P()),
        check_vma=False,
    )
```

```python
import functools

import jax
import jax.numpy as jnp
from jax import lax
from jax.experimental import pallas as pl
from jax.experimental.pallas import tpu as pltpu
from jax.sharding import PartitionSpec as P

OWN_DEV = 2048
HUBS = 1024
FANOUT = 5
CAP = 18
MAIN = 16
REST = CAP - MAIN
FRONT = 80
CHUNK = 112
GROUP = 16
VMEM_LIMIT = 28 * 1024 * 1024
BF = jnp.bfloat16
F32 = jnp.float32
I32 = jnp.int32


def mm(a, b):
    return jnp.dot(a, b, preferred_element_type=F32)


def mm_nt(a, b):
    return lax.dot_general(a, b, (((1,), (1,)), ((), ())), preferred_element_type=F32)


def mm_tn(a, b):
    return lax.dot_general(a, b, (((0,), (0,)), ((), ())), preferred_element_type=F32)


def onehot(flag):
    return jnp.where(flag, 1.0, 0.0).astype(BF)


def slot_kinds(me, slot, named, ranks):
    t = named[0].shape[1]
    lane = lax.broadcasted_iota(I32, (256, t), 0)
    at_main = (me % 8) * MAIN
    at_rest = (me % 64) * REST - MAIN + 128
    values, lanes = [], []
    for j, rank in enumerate(ranks):
        value = slot[j]
        high, low = (value // 64).astype(F32), (value % 64).astype(F32)
        values.append(
            jnp.concatenate(
                [jnp.where(named[j], high, 0.0), jnp.where(named[j], low, 0.0)], axis=0
            ).astype(BF)
        )
        lanes.append(onehot(lane == rank + jnp.where(rank < MAIN, at_main, at_rest)))
    return mm_nt(jnp.concatenate(values, axis=1), jnp.concatenate(lanes, axis=1))


def grads_kernel(
    me, h_in, a_in, go_in, ws_in, wn_in, owner_in, slot_in, hub_in,
    grad_self, message, mine, send, places, kinds,
    h, a, go, ws, wn, owner, slot, hub, back, arrived,
):
    loads = [
        pltpu.make_async_copy(src, dst, arrived.at[i])
        for i, (src, dst) in enumerate(
            (
                (owner_in, owner), (slot_in, slot), (hub_in, hub),
                (h_in, h), (ws_in, ws), (a_in, a), (wn_in, wn), (go_in, go),
            )
        )
    ]
    for load in loads:
        load.start()

    t = h.shape[0]
    n = kinds.shape[1]
    fan = slot.shape[0]
    device = lax.broadcasted_iota(I32, (n, t), 0)
    before = onehot(lax.broadcasted_iota(I32, (t, t), 0) < lax.broadcasted_iota(I32, (t, t), 1))
    loads[0].wait()
    loads[1].wait()
    named = [device == owner[j] for j in range(fan)]
    slots = [slot[j : j + 1, :] for j in range(fan)]
    hot = jnp.concatenate([onehot(f) for f in named], axis=0)
    earlier = mm(hot, before)
    amount = jnp.sum(hot.astype(F32), axis=1, keepdims=True)
    base = jnp.zeros((n, 1), F32)
    ranks = []
    for j in range(fan):
        rank = jnp.where(named[j], earlier[j * n : (j + 1) * n, :] + base, 0.0)
        ranks.append(jnp.sum(rank, axis=0, keepdims=True).astype(I32))
        base = base + amount[j * n : (j + 1) * n, :]
    for j in range(fan):
        in_main = ranks[j] < MAIN
        places[j : j + 1, :] = jnp.where(in_main, owner[j] * MAIN + ranks[j], -1)
        places[4 + j : 5 + j, :] = jnp.where(in_main, -1, owner[j] * REST + (ranks[j] - MAIN))
    kind = slot_kinds(me[0], slots, named, ranks).astype(BF)
    for i in range(4):
        kinds[i] = kind[(i % 2) * n : (i % 2 + 1) * n, (i // 2) * 128 : (i // 2 + 1) * 128]
    loads[2].wait()
    rows = lax.broadcasted_iota(I32, (HUBS, t), 0)
    count = onehot(rows == hub[0:1, :]) + onehot(rows == hub[1:2, :])

    loads[3].wait()
    loads[4].wait()
    pre = mm(h[...], ws[...])
    loads[5].wait()
    loads[6].wait()
    pre = pre + mm(a[...], wn[...])
    loads[7].wait()
    sig = jax.nn.sigmoid(pre)
    g = (go[...].astype(F32) * (sig * (1.0 + pre * (1.0 - sig)))).astype(BF)
    back[...] = mm_nt(g, ws[...]).astype(BF)
    store = pltpu.make_async_copy(back, grad_self, arrived.at[8])
    store.start()
    msg = (mm_nt(g, wn[...]) / FANOUT).astype(BF)
    message[...] = msg
    hub_part = mm(count, msg).astype(BF)
    depth = h.shape[1]
    first = lax.rem(me[0], 2) == 0
    part_self = mm_tn(h[...], g).astype(BF)
    part_neigh = mm_tn(a[...], g).astype(BF)

    @pl.when(first)
    def _():
        mine[...] = hub_part
        send[0:depth, :] = part_self
        send[depth : 2 * depth, :] = part_neigh

    @pl.when(jnp.logical_not(first))
    def _():
        send[...] = hub_part
        mine[0:depth, :] = part_self
        mine[depth : 2 * depth, :] = part_neigh

    store.wait()


def spread_rows():
    row = lax.broadcasted_iota(I32, (GROUP * 16, 192), 0)
    col = lax.broadcasted_iota(I32, (GROUP * 16, 192), 1)
    chunk, s = row // 16, row % 16
    want = jnp.where(s < 8, (s // 2) * 32 + chunk * 2 + s % 2, 128 + (s - 8) * 16 + chunk)
    return onehot((s < 12) & (col == want))


def picks(places, first, at):
    flag = at == places[first : first + 1, :]
    for j in range(first + 1, first + 3):
        flag = flag | (at == places[j : j + 1, :])
    return onehot(flag)


def pack_kernel(places, kinds, message, out):
    t = message.shape[0]
    chunks = out.shape[0]
    spread = spread_rows()
    msg = message[...]
    at = lax.broadcasted_iota(I32, (chunks * MAIN, t), 0)
    rows = mm(picks(places, 0, at), msg).astype(BF)
    for q in range(4):
        out[:, q * 16 : (q + 1) * 16, :] = rows[:, q * 128 : (q + 1) * 128].reshape(
            chunks, 16, 128
        )
    at = lax.broadcasted_iota(I32, (chunks * REST, t), 0)
    rest = mm(picks(places, 4, at), msg).astype(BF)
    for g in range(chunks // GROUP):
        stacked = jnp.concatenate(
            [rest[g * 32 : (g + 1) * 32, q * 128 : (q + 1) * 128] for q in range(4)]
            + [kinds[i, g * GROUP : (g + 1) * GROUP, :] for i in range(4)],
            axis=0,
        )
        out[g * GROUP : (g + 1) * GROUP, 64:80, :] = (
            mm(spread, stacked).astype(BF).reshape(GROUP, 16, 128)
        )


def join_kernel(mine, got, held, out):
    for half in range(2):
        for q in range(2):
            at = half * 256 + q * 128
            total = mine[:, at : at + 128].astype(F32) + got[:, at : at + 128].astype(F32)
            first = FRONT + q * 16
            out[:, half, first : first + 16, :] = total.astype(BF).reshape(-1, 16, 128)


def reduce_kernel(received, out, parts, total, arrived, left):
    chips = parts.shape[0]
    steps, copies = arrived.shape[0], left.shape[0]
    piece, each = chips // steps, total.shape[0]
    loads = [
        pltpu.make_async_copy(
            received.at[pl.ds(i * piece, piece), :, pl.ds(FRONT, 32), :],
            parts.at[pl.ds(i * piece, piece)],
            arrived.at[i],
        )
        for i in range(steps)
    ]
    for load in loads:
        load.start()
    acc = jnp.zeros((1, 2, 32, 128), F32)
    for i, load in enumerate(loads):
        load.wait()
        block = parts[i * piece : (i + 1) * piece].astype(F32)
        acc = acc + jnp.sum(block, axis=0, keepdims=True)
    total[...] = jnp.broadcast_to(acc.astype(BF), total.shape)
    stores = [
        pltpu.make_async_copy(total, out.at[pl.ds(i * each, each)], left.at[i])
        for i in range(copies)
    ]
    for store in stores:
        store.start()
    for store in stores:
        store.wait()


def front_kernel(received, out, rows, index):
    step = pl.program_id(0)
    n = received.shape[0]

    @pl.when(step == 0)
    def _():
        for q in range(4):
            rows[0 : n * MAIN, q * 128 : (q + 1) * 128] = received[
                :, q * 16 : (q + 1) * 16, :
            ].reshape(n * MAIN, 128)
        spread = spread_rows()
        main = []
        rest = [jnp.zeros((1, 128), F32), jnp.zeros((1, 128), F32)]
        for k in range(n // GROUP):
            tile = received[k * GROUP : (k + 1) * GROUP, 64:80, :].reshape(GROUP * 16, 128)
            stacked = mm_tn(spread, tile)
            for q in range(4):
                rows[n * MAIN + k * 32 : n * MAIN + (k + 1) * 32, q * 128 : (q + 1) * 128] = (
                    stacked[q * 32 : (q + 1) * 32, :].astype(BF)
                )
            main_slot = stacked[128:144, :] * 64.0 + stacked[144:160, :]
            rest_slot = stacked[160:176, :] * 64.0 + stacked[176:192, :]
            main.append(jnp.sum(main_slot[0:8, :], axis=0, keepdims=True))
            main.append(jnp.sum(main_slot[8:16, :], axis=0, keepdims=True))
            part = k * GROUP // 64
            rest[part] = rest[part] + jnp.sum(rest_slot, axis=0, keepdims=True)
        for g, line in enumerate(main + rest):
            index[g : g + 1, :] = line.astype(I32)

    block = out.shape[0]
    wanted = lax.broadcasted_iota(I32, (block, 128), 0) + step * block
    hot = jnp.concatenate(
        [onehot(wanted == index[g : g + 1, :]) for g in range(n * CAP // 128)], axis=1
    )
    out[...] = mm(hot, rows[...])


def fill_kernel(scale, mine, me, part, *refs):
    hub_grad, grad_w_self, grad_w_neigh, wide, done = refs[-5:]
    depth = grad_w_self.shape[0]
    hubs = (lax.rem(me[0], 2) == 0) == mine
    factor = jnp.where(hubs, 1.0, scale)
    steps = 4
    rows = HUBS // steps
    chips = rows // 16

    def copies(step):
        src = wide.at[pl.ds(step * rows, rows)]
        to_hubs = hub_grad.at[pl.ds(step * rows, rows)]
        weights = grad_w_self if step < steps // 2 else grad_w_neigh
        to_weights = weights.at[pl.ds(step * rows % depth, rows)]
        return (
            pltpu.make_async_copy(src, to_hubs, done.at[step]),
            pltpu.make_async_copy(src, to_weights, done.at[step]),
        )

    for step in range(steps):
        for half in range(2):
            for q in range(2):
                at = half * 256 + q * 128
                block = part[step * chips : (step + 1) * chips, half, q * 16 : (q + 1) * 16, :]
                wide[step * rows : (step + 1) * rows, at : at + 128] = (
                    block.reshape(rows, 128).astype(F32) * factor
                )
        to_hubs, to_weights = copies(step)
        pl.when(hubs)(to_hubs.start)
        pl.when(jnp.logical_not(hubs))(to_weights.start)
    for step in range(steps):
        to_hubs, to_weights = copies(step)
        pl.when(hubs)(to_hubs.wait)
        pl.when(jnp.logical_not(hubs))(to_weights.wait)


SMEM = pl.BlockSpec(memory_space=pltpu.SMEM)
HBM = pl.BlockSpec(memory_space=pltpu.HBM)
VMEM = pl.BlockSpec(memory_space=pltpu.VMEM)
PARAMS = pltpu.CompilerParams(vmem_limit_bytes=VMEM_LIMIT)


def in_hbm(x):
    return pltpu.with_memory_space_constraint(x, pltpu.HBM)


def in_vmem(x):
    return pltpu.with_memory_space_constraint(x, pltpu.VMEM)


def body(h_self, agg, grad_out, w_self, w_neigh, owner, slot, hub_refs):
    t, width = h_self.shape
    n = lax.axis_size("dev")
    me = lax.axis_index("dev").astype(I32).reshape(1)
    owner_t = owner.transpose(1, 2, 0)
    slot_t = slot.T
    hub_t = hub_refs.T
    swap = [(i, i ^ 1) for i in range(n)]
    half = jax.ShapeDtypeStruct((HUBS, width), BF)
    same = jax.ShapeDtypeStruct((t, width), BF)

    fan = slot.shape[1]
    with jax.named_scope("grads"):
        grad_self, message, mine, send, places, kinds = pl.pallas_call(
            grads_kernel,
            out_shape=(
                pltpu.HBM((t, width), BF),
                pltpu.VMEM((t, width), BF),
                pltpu.VMEM((HUBS, width), BF),
                pltpu.VMEM((HUBS, width), BF),
                pltpu.VMEM((8, t), I32),
                pltpu.VMEM((4, n, 128), BF),
            ),
            in_specs=[SMEM] + [HBM] * 8,
            out_specs=[HBM] + [VMEM] * 5,
            scratch_shapes=[pltpu.VMEM((t, width), BF)] * 3
            + [pltpu.VMEM((width, width), BF)] * 2
            + [
                pltpu.VMEM((fan, 1, t), I32),
                pltpu.VMEM((fan, t), I32),
                pltpu.VMEM(hub_t.shape, I32),
                pltpu.VMEM((t, width), BF),
                pltpu.SemaphoreType.DMA((9,)),
            ],
            compiler_params=PARAMS,
        )(me, *map(in_hbm, (h_self, agg, grad_out, w_self, w_neigh, owner_t, slot_t, hub_t)))
    with jax.named_scope("core_exchange"):
        got = lax.ppermute(send, "dev", swap)
    with jax.named_scope("pack"):
        packed = pl.pallas_call(
            pack_kernel,
            out_shape=pltpu.VMEM((n, CHUNK, 128), BF),
            in_specs=[VMEM] * 3,
            out_specs=VMEM,
            compiler_params=PARAMS,
        )(*map(in_vmem, (places, kinds, message)))
    with jax.named_scope("join"):
        packed = pl.pallas_call(
            join_kernel,
            out_shape=pltpu.VMEM((n // 2, 2, CHUNK, 128), BF),
            in_specs=[VMEM, VMEM, HBM],
            out_specs=VMEM,
            input_output_aliases={2: 0},
            compiler_params=PARAMS,
        )(in_vmem(mine), in_vmem(got), in_vmem(packed.reshape(n // 2, 2, CHUNK, 128)))
    with jax.named_scope("rows_to_owners"):
        received = lax.all_to_all(
            packed.reshape(n, CHUNK, 128), "dev", split_axis=0, concat_axis=0, tiled=True
        )
    with jax.named_scope("sum_parts"):
        total = pl.pallas_call(
            reduce_kernel,
            out_shape=pltpu.HBM((n // 2, 2, 32, 128), BF),
            in_specs=[HBM],
            out_specs=HBM,
            scratch_shapes=[
                pltpu.VMEM((n // 2, 2, 32, 128), BF),
                pltpu.VMEM((8, 2, 32, 128), BF),
                pltpu.SemaphoreType.DMA((4,)),
                pltpu.SemaphoreType.DMA((n // 16,)),
            ],
            compiler_params=PARAMS,
        )(in_hbm(received.reshape(n // 2, 2, CHUNK, 128)))
    with jax.named_scope("sums_to_all"):
        own = lax.all_to_all(
            total.reshape(n, 32, 128), "dev", split_axis=0, concat_axis=0, tiled=True
        )
    with jax.named_scope("front"):
        front_grad = pl.pallas_call(
            front_kernel,
            out_shape=jax.ShapeDtypeStruct((OWN_DEV, width), F32),
            grid=(8,),
            in_specs=[pl.BlockSpec((n, FRONT, 128), lambda i: (0, 0, 0))],
            out_specs=pl.BlockSpec((OWN_DEV // 8, width), lambda i: (i, 0)),
            scratch_shapes=[
                pltpu.VMEM((n * CAP, width), BF),
                pltpu.VMEM((24, 128), I32),
            ],
            compiler_params=PARAMS,
            cost_estimate=pl.CostEstimate(
                flops=2 * OWN_DEV * n * CAP * width, bytes_accessed=8 << 20, transcendentals=0
            ),
        )(in_hbm(received))
    own, front_grad = lax.optimization_barrier((own, front_grad))
    with jax.named_scope("core_exchange_back"):
        other = lax.ppermute(own, "dev", swap)
    scale = 1.0 / (t * n) ** 0.5
    filled = ()
    for mine_too, part in ((True, own), (False, other)):
        with jax.named_scope("fill_own" if mine_too else "fill_other"):
            filled = pl.pallas_call(
                functools.partial(fill_kernel, scale, mine_too),
                out_shape=(
                    jax.ShapeDtypeStruct((HUBS, width), F32),
                    jax.ShapeDtypeStruct((width, width), F32),
                    jax.ShapeDtypeStruct((width, width), F32),
                ),
                in_specs=[SMEM, VMEM] + [HBM] * len(filled),
                out_specs=[HBM] * 3,
                scratch_shapes=[pltpu.VMEM((HUBS, width), F32), pltpu.SemaphoreType.DMA((4,))],
                input_output_aliases={2 + i: i for i in range(len(filled))},
                compiler_params=PARAMS,
                cost_estimate=pl.CostEstimate(
                    flops=HUBS * width, bytes_accessed=3 << 20, transcendentals=0
                ),
            )(me, part.reshape(n // 2, 2, 32, 128), *filled)
    hub_grad, grad_w_self, grad_w_neigh = filled
    return grad_self, front_grad, hub_grad, grad_w_self, grad_w_neigh


def solution(mesh):
    placed = (
        P("dev", None),
        P("dev", None),
        P("dev", None),
        P(),
        P(),
        P("dev", None, None),
        P("dev", None),
        P("dev", None),
    )
    return jax.shard_map(
        body,
        mesh=mesh,
        in_specs=placed,
        out_specs=(P("dev", None), P("dev", None), P(), P(), P()),
        check_vma=False,
    )
```

```python
import functools

import jax
import jax.numpy as jnp
from jax import lax
from jax.experimental import pallas as pl
from jax.experimental.pallas import tpu as pltpu
from jax.sharding import PartitionSpec as P

OWN_DEV = 2048
HUBS = 1024
FANOUT = 5
CAP = 18
MAIN = 16
REST = CAP - MAIN
FRONT = 80
CHUNK = 112
GROUP = 16
VMEM_LIMIT = 28 * 1024 * 1024
BF = jnp.bfloat16
F32 = jnp.float32
I32 = jnp.int32
I16 = jnp.int16


def mm(a, b):
    return jnp.dot(a, b, preferred_element_type=F32)


def mm_nt(a, b):
    return lax.dot_general(a, b, (((1,), (1,)), ((), ())), preferred_element_type=F32)


def mm_tn(a, b):
    return lax.dot_general(a, b, (((0,), (0,)), ((), ())), preferred_element_type=F32)


def onehot(flag):
    return jnp.where(flag, jnp.ones((), BF), jnp.zeros((), BF))


def slot_kinds(me, slot, hots, ranks):
    t = slot.shape[1]
    row = lax.broadcasted_iota(I32, (32, t), 0)
    values = []
    for j, rank in enumerate(ranks):
        value = slot[j : j + 1, :]
        at = row == rank
        high = jnp.where(at, (value // 64).astype(F32), 0.0)
        low = jnp.where(at, (value % 64).astype(F32), 0.0)
        values.append(jnp.concatenate([high, low], axis=0).astype(BF))
    by_rank = mm_nt(jnp.concatenate(hots, axis=1), jnp.concatenate(values, axis=1)).astype(BF)
    source = lax.broadcasted_iota(I32, (64, 512), 0)
    target = lax.broadcasted_iota(I32, (64, 512), 1)
    rank, part = source % 32, source // 32
    in_main = rank < MAIN
    lane = jnp.where(in_main, (me % 8) * MAIN + rank, (me % 64) * REST + rank - MAIN)
    kind = jnp.where(in_main, 0, 2) + part
    return mm(by_rank, onehot((rank < CAP) & (target == kind * 128 + lane)))


def grads_kernel(
    me, h_in, a_in, go_in, ws_in, wn_in, hub_in, owner_in, slot_in,
    grad_self, message, mine, send, owner, slot,
    h, a, go, ws, wn, hub, back, arrived,
):
    loads = [
        pltpu.make_async_copy(src, dst, arrived.at[i])
        for i, (src, dst) in enumerate(
            (
                (h_in, h), (ws_in, ws), (a_in, a), (wn_in, wn), (go_in, go), (hub_in, hub),
                (owner_in, owner), (slot_in, slot),
            )
        )
    ]
    for load in loads:
        load.start()

    t = h.shape[0]
    loads[0].wait()
    loads[1].wait()
    pre = mm(h[...], ws[...])
    loads[2].wait()
    loads[3].wait()
    pre = pre + mm(a[...], wn[...])
    loads[4].wait()
    sig = jax.nn.sigmoid(pre)
    g = (go[...].astype(F32) * (sig * (1.0 + pre * (1.0 - sig)))).astype(BF)
    back[...] = mm_nt(g, ws[...]).astype(BF)
    store = pltpu.make_async_copy(back, grad_self, arrived.at[8])
    store.start()
    msg = (mm_nt(g, wn[...]) / FANOUT).astype(BF)
    message[...] = msg
    loads[5].wait()
    rows = lax.broadcasted_iota(I16, (HUBS, t), 0)
    ids = hub[...].astype(I16)
    count = onehot(rows == ids[0:1, :]) + onehot(rows == ids[1:2, :])
    hub_part = mm(count, msg).astype(BF)
    depth = h.shape[1]
    first = lax.rem(me[0], 2) == 0
    part_self = mm_tn(h[...], g).astype(BF)
    part_neigh = mm_tn(a[...], g).astype(BF)

    @pl.when(first)
    def _():
        mine[...] = hub_part
        send[0:depth, :] = part_self
        send[depth : 2 * depth, :] = part_neigh

    @pl.when(jnp.logical_not(first))
    def _():
        send[...] = hub_part
        mine[0:depth, :] = part_self
        mine[depth : 2 * depth, :] = part_neigh

    store.wait()
    loads[6].wait()
    loads[7].wait()


def spread_rows():
    row = lax.broadcasted_iota(I32, (GROUP * 16, 192), 0)
    col = lax.broadcasted_iota(I32, (GROUP * 16, 192), 1)
    chunk, s = row // 16, row % 16
    want = jnp.where(s < 8, (s // 2) * 32 + chunk * 2 + s % 2, 128 + (s - 8) * 16 + chunk)
    return onehot((s < 12) & (col == want))


def picks(places, at):
    return onehot((at == places[0]) | (at == places[1]) | (at == places[2]))


def pack_kernel(me, owner, slot, message, out):
    t = message.shape[0]
    n = out.shape[0]
    fan = slot.shape[0]
    device = lax.broadcasted_iota(I32, (n, t), 0)
    before = onehot(
        lax.broadcasted_iota(I16, (t, t), 0) < lax.broadcasted_iota(I16, (t, t), 1)
    )
    named = [device == owner[j] for j in range(fan)]
    hots = [onehot(f) for f in named]
    hot = jnp.concatenate(hots, axis=0)
    earlier = mm(hot, before)
    amount = jnp.sum(hot.astype(F32), axis=1, keepdims=True)
    base = jnp.zeros((n, 1), F32)
    ranks = []
    for j in range(fan):
        rank = jnp.where(named[j], earlier[j * n : (j + 1) * n, :] + base, 0.0)
        ranks.append(jnp.sum(rank, axis=0, keepdims=True).astype(I32))
        base = base + amount[j * n : (j + 1) * n, :]
    main, last = [], []
    for j, rank in enumerate(ranks):
        in_main = rank < MAIN
        main.append(jnp.where(in_main, owner[j] * MAIN + rank, -1).astype(I16))
        last.append(jnp.where(in_main, -1, owner[j] * REST + (rank - MAIN)).astype(I16))
    kinds = slot_kinds(me[0], slot[...], hots, ranks).astype(BF)

    msg = message[...]
    spread = spread_rows()
    rest = mm(picks(last, lax.broadcasted_iota(I16, (n * REST, t), 0)), msg).astype(BF)
    for g in range(n // GROUP):
        stacked = jnp.concatenate(
            [rest[g * 32 : (g + 1) * 32, q * 128 : (q + 1) * 128] for q in range(4)]
            + [kinds[g * GROUP : (g + 1) * GROUP, q * 128 : (q + 1) * 128] for q in range(4)],
            axis=0,
        )
        out[g * GROUP : (g + 1) * GROUP, 64:80, :] = (
            mm(spread, stacked).astype(BF).reshape(GROUP, 16, 128)
        )
    rows = mm(picks(main, lax.broadcasted_iota(I16, (n * MAIN, t), 0)), msg).astype(BF)
    for q in range(4):
        out[:, q * 16 : (q + 1) * 16, :] = rows[:, q * 128 : (q + 1) * 128].reshape(n, 16, 128)


def join_kernel(mine, got, held, out):
    for half in range(2):
        for q in range(2):
            at = half * 256 + q * 128
            total = mine[:, at : at + 128].astype(F32) + got[:, at : at + 128].astype(F32)
            first = FRONT + q * 16
            out[:, half, first : first + 16, :] = total.astype(BF).reshape(-1, 16, 128)


def reduce_kernel(received, out, parts, total, arrived, left):
    chips = parts.shape[0]
    steps, copies = arrived.shape[0], left.shape[0]
    piece, each = chips // steps, total.shape[0]
    loads = [
        pltpu.make_async_copy(
            received.at[pl.ds(i * piece, piece), :, pl.ds(FRONT, 32), :],
            parts.at[pl.ds(i * piece, piece)],
            arrived.at[i],
        )
        for i in range(steps)
    ]
    for load in loads:
        load.start()
    acc = jnp.zeros((1, 2, 32, 128), F32)
    for i, load in enumerate(loads):
        load.wait()
        block = parts[i * piece : (i + 1) * piece].astype(F32)
        acc = acc + jnp.sum(block, axis=0, keepdims=True)
    total[...] = jnp.broadcast_to(acc.astype(BF), total.shape)
    stores = [
        pltpu.make_async_copy(total, out.at[pl.ds(i * each, each)], left.at[i])
        for i in range(copies)
    ]
    for store in stores:
        store.start()
    for store in stores:
        store.wait()


def front_kernel(received, out, rows, index):
    step = pl.program_id(0)
    n = received.shape[0]

    @pl.when(step == 0)
    def _():
        for q in range(4):
            rows[0 : n * MAIN, q * 128 : (q + 1) * 128] = received[
                :, q * 16 : (q + 1) * 16, :
            ].reshape(n * MAIN, 128)
        spread = spread_rows()
        main = []
        rest = [jnp.zeros((1, 128), F32), jnp.zeros((1, 128), F32)]
        for k in range(n // GROUP):
            tile = received[k * GROUP : (k + 1) * GROUP, 64:80, :].reshape(GROUP * 16, 128)
            stacked = mm_tn(spread, tile)
            for q in range(4):
                rows[n * MAIN + k * 32 : n * MAIN + (k + 1) * 32, q * 128 : (q + 1) * 128] = (
                    stacked[q * 32 : (q + 1) * 32, :].astype(BF)
                )
            main_slot = stacked[128:144, :] * 64.0 + stacked[144:160, :]
            rest_slot = stacked[160:176, :] * 64.0 + stacked[176:192, :]
            main.append(jnp.sum(main_slot[0:8, :], axis=0, keepdims=True))
            main.append(jnp.sum(main_slot[8:16, :], axis=0, keepdims=True))
            part = k * GROUP // 64
            rest[part] = rest[part] + jnp.sum(rest_slot, axis=0, keepdims=True)
        for g, line in enumerate(main + rest):
            index[g : g + 1, :] = line.astype(I32)

    block = out.shape[0]
    wanted = lax.broadcasted_iota(I32, (block, 128), 0) + step * block
    hot = jnp.concatenate(
        [onehot(wanted == index[g : g + 1, :]) for g in range(n * CAP // 128)], axis=1
    )
    out[...] = mm(hot, rows[...])


def fill_kernel(scale, mine, me, part, *refs):
    hub_grad, grad_w_self, grad_w_neigh, wide, done = refs[-5:]
    depth = grad_w_self.shape[0]
    hubs = (lax.rem(me[0], 2) == 0) == mine
    factor = jnp.where(hubs, 1.0, scale)
    steps = 4
    rows = HUBS // steps
    chips = rows // 16

    def copies(step):
        src = wide.at[pl.ds(step * rows, rows)]
        to_hubs = hub_grad.at[pl.ds(step * rows, rows)]
        weights = grad_w_self if step < steps // 2 else grad_w_neigh
        to_weights = weights.at[pl.ds(step * rows % depth, rows)]
        return (
            pltpu.make_async_copy(src, to_hubs, done.at[step]),
            pltpu.make_async_copy(src, to_weights, done.at[step]),
        )

    for step in range(steps):
        for half in range(2):
            for q in range(2):
                at = half * 256 + q * 128
                block = part[step * chips : (step + 1) * chips, half, q * 16 : (q + 1) * 16, :]
                wide[step * rows : (step + 1) * rows, at : at + 128] = (
                    block.reshape(rows, 128).astype(F32) * factor
                )
        to_hubs, to_weights = copies(step)
        pl.when(hubs)(to_hubs.start)
        pl.when(jnp.logical_not(hubs))(to_weights.start)
    for step in range(steps):
        to_hubs, to_weights = copies(step)
        pl.when(hubs)(to_hubs.wait)
        pl.when(jnp.logical_not(hubs))(to_weights.wait)


SMEM = pl.BlockSpec(memory_space=pltpu.SMEM)
HBM = pl.BlockSpec(memory_space=pltpu.HBM)
VMEM = pl.BlockSpec(memory_space=pltpu.VMEM)
PARAMS = pltpu.CompilerParams(vmem_limit_bytes=VMEM_LIMIT)


def in_hbm(x):
    return pltpu.with_memory_space_constraint(x, pltpu.HBM)


def in_vmem(x):
    return pltpu.with_memory_space_constraint(x, pltpu.VMEM)


def body(h_self, agg, grad_out, w_self, w_neigh, owner, slot, hub_refs):
    t, width = h_self.shape
    n = lax.axis_size("dev")
    me = lax.axis_index("dev").astype(I32).reshape(1)
    owner_t = owner.transpose(1, 2, 0)
    slot_t = slot.T
    hub_t = hub_refs.T
    swap = [(i, i ^ 1) for i in range(n)]

    with jax.named_scope("grads"):
        grad_self, message, mine, send, owner_v, slot_v = pl.pallas_call(
            grads_kernel,
            out_shape=(
                pltpu.HBM((t, width), BF),
                pltpu.VMEM((t, width), BF),
                pltpu.VMEM((HUBS, width), BF),
                pltpu.VMEM((HUBS, width), BF),
                pltpu.VMEM(owner_t.shape, I32),
                pltpu.VMEM(slot_t.shape, I32),
            ),
            in_specs=[SMEM] + [HBM] * 8,
            out_specs=[HBM] + [VMEM] * 5,
            scratch_shapes=[pltpu.VMEM((t, width), BF)] * 3
            + [pltpu.VMEM((width, width), BF)] * 2
            + [
                pltpu.VMEM(hub_t.shape, I32),
                pltpu.VMEM((t, width), BF),
                pltpu.SemaphoreType.DMA((9,)),
            ],
            compiler_params=PARAMS,
        )(me, *map(in_hbm, (h_self, agg, grad_out, w_self, w_neigh, hub_t, owner_t, slot_t)))
    with jax.named_scope("core_exchange"):
        got = lax.ppermute(send, "dev", swap)
    with jax.named_scope("pack"):
        packed = pl.pallas_call(
            pack_kernel,
            out_shape=pltpu.VMEM((n, CHUNK, 128), BF),
            in_specs=[SMEM] + [VMEM] * 3,
            out_specs=VMEM,
            compiler_params=PARAMS,
        )(me, *map(in_vmem, (owner_v, slot_v, message)))
    with jax.named_scope("join"):
        packed = pl.pallas_call(
            join_kernel,
            out_shape=pltpu.VMEM((n // 2, 2, CHUNK, 128), BF),
            in_specs=[VMEM, VMEM, HBM],
            out_specs=VMEM,
            input_output_aliases={2: 0},
            compiler_params=PARAMS,
        )(in_vmem(mine), in_vmem(got), in_vmem(packed.reshape(n // 2, 2, CHUNK, 128)))
    with jax.named_scope("rows_to_owners"):
        received = lax.all_to_all(
            packed.reshape(n, CHUNK, 128), "dev", split_axis=0, concat_axis=0, tiled=True
        )
    with jax.named_scope("sum_parts"):
        total = pl.pallas_call(
            reduce_kernel,
            out_shape=pltpu.HBM((n // 2, 2, 32, 128), BF),
            in_specs=[HBM],
            out_specs=HBM,
            scratch_shapes=[
                pltpu.VMEM((n // 2, 2, 32, 128), BF),
                pltpu.VMEM((8, 2, 32, 128), BF),
                pltpu.SemaphoreType.DMA((4,)),
                pltpu.SemaphoreType.DMA((n // 16,)),
            ],
            compiler_params=PARAMS,
        )(in_hbm(received.reshape(n // 2, 2, CHUNK, 128)))
    with jax.named_scope("sums_to_all"):
        own = lax.all_to_all(
            total.reshape(n, 32, 128), "dev", split_axis=0, concat_axis=0, tiled=True
        )
    with jax.named_scope("front"):
        front_grad = pl.pallas_call(
            front_kernel,
            out_shape=jax.ShapeDtypeStruct((OWN_DEV, width), F32),
            grid=(8,),
            in_specs=[pl.BlockSpec((n, FRONT, 128), lambda i: (0, 0, 0))],
            out_specs=pl.BlockSpec((OWN_DEV // 8, width), lambda i: (i, 0)),
            scratch_shapes=[
                pltpu.VMEM((n * CAP, width), BF),
                pltpu.VMEM((24, 128), I32),
            ],
            compiler_params=PARAMS,
            cost_estimate=pl.CostEstimate(
                flops=2 * OWN_DEV * n * CAP * width, bytes_accessed=8 << 20, transcendentals=0
            ),
        )(in_hbm(received))
    own, front_grad = lax.optimization_barrier((own, front_grad))
    with jax.named_scope("core_exchange_back"):
        other = lax.ppermute(own, "dev", swap)
    scale = 1.0 / (t * n) ** 0.5
    filled = ()
    for mine_too, part in ((True, own), (False, other)):
        with jax.named_scope("fill_own" if mine_too else "fill_other"):
            filled = pl.pallas_call(
                functools.partial(fill_kernel, scale, mine_too),
                out_shape=(
                    jax.ShapeDtypeStruct((HUBS, width), F32),
                    jax.ShapeDtypeStruct((width, width), F32),
                    jax.ShapeDtypeStruct((width, width), F32),
                ),
                in_specs=[SMEM, VMEM] + [HBM] * len(filled),
                out_specs=[HBM] * 3,
                scratch_shapes=[pltpu.VMEM((HUBS, width), F32), pltpu.SemaphoreType.DMA((4,))],
                input_output_aliases={2 + i: i for i in range(len(filled))},
                compiler_params=PARAMS,
                cost_estimate=pl.CostEstimate(
                    flops=HUBS * width, bytes_accessed=3 << 20, transcendentals=0
                ),
            )(me, part.reshape(n // 2, 2, 32, 128), *filled)
    hub_grad, grad_w_self, grad_w_neigh = filled
    return grad_self, front_grad, hub_grad, grad_w_self, grad_w_neigh


def solution(mesh):
    placed = (
        P("dev", None),
        P("dev", None),
        P("dev", None),
        P(),
        P(),
        P("dev", None, None),
        P("dev", None),
        P("dev", None),
    )
    return jax.shard_map(
        body,
        mesh=mesh,
        in_specs=placed,
        out_specs=(P("dev", None), P("dev", None), P(), P(), P()),
        check_vma=False,
    )
```

```python
import functools

import jax
import jax.numpy as jnp
from jax import lax
from jax.experimental import pallas as pl
from jax.experimental.pallas import tpu as pltpu
from jax.sharding import PartitionSpec as P

OWN_DEV = 2048
HUBS = 1024
FANOUT = 5
CAP = 18
MAIN = 16
REST = CAP - MAIN
FRONT = 80
CHUNK = 112
GROUP = 16
VMEM_LIMIT = 28 * 1024 * 1024
BF = jnp.bfloat16
F32 = jnp.float32
I32 = jnp.int32
I16 = jnp.int16


def mm(a, b):
    return jnp.dot(a, b, preferred_element_type=F32)


def mm_nt(a, b):
    return lax.dot_general(a, b, (((1,), (1,)), ((), ())), preferred_element_type=F32)


def mm_tn(a, b):
    return lax.dot_general(a, b, (((0,), (0,)), ((), ())), preferred_element_type=F32)


def onehot(flag):
    return jnp.where(flag, jnp.ones((), BF), jnp.zeros((), BF))


def slot_kinds(me, slot, hots, ranks):
    t = slot.shape[1]
    row = lax.broadcasted_iota(I32, (32, t), 0)
    values = []
    for j, rank in enumerate(ranks):
        value = slot[j : j + 1, :]
        at = row == rank
        high = jnp.where(at, (value // 64).astype(F32), 0.0)
        low = jnp.where(at, (value % 64).astype(F32), 0.0)
        values.append(jnp.concatenate([high, low], axis=0).astype(BF))
    by_rank = mm_nt(jnp.concatenate(hots, axis=1), jnp.concatenate(values, axis=1)).astype(BF)
    source = lax.broadcasted_iota(I32, (64, 512), 0)
    target = lax.broadcasted_iota(I32, (64, 512), 1)
    rank, part = source % 32, source // 32
    in_main = rank < MAIN
    lane = jnp.where(in_main, (me % 8) * MAIN + rank, (me % 64) * REST + rank - MAIN)
    kind = jnp.where(in_main, 0, 2) + part
    return mm(by_rank, onehot((rank < CAP) & (target == kind * 128 + lane)))


def grads_kernel(
    me, h_in, a_in, go_in, ws_in, wn_in, hub_in, owner_in, slot_in,
    g_out, message, mine, send, owner, slot,
    h, a, go, ws, wn, hub, g, arrived,
):
    loads = [
        pltpu.make_async_copy(src, dst, arrived.at[i])
        for i, (src, dst) in enumerate(
            (
                (h_in, h), (ws_in, ws), (a_in, a), (wn_in, wn), (go_in, go), (hub_in, hub),
                (owner_in, owner), (slot_in, slot),
            )
        )
    ]
    for load in loads:
        load.start()

    t = h.shape[0]
    loads[0].wait()
    loads[1].wait()
    pre = mm(h[...], ws[...])
    loads[2].wait()
    loads[3].wait()
    pre = pre + mm(a[...], wn[...])
    loads[4].wait()
    sig = jax.nn.sigmoid(pre)
    g[...] = (go[...].astype(F32) * (sig * (1.0 + pre * (1.0 - sig)))).astype(BF)
    store = pltpu.make_async_copy(g, g_out, arrived.at[8])
    store.start()
    msg = (mm_nt(g[...], wn[...]) / FANOUT).astype(BF)
    message[...] = msg
    loads[5].wait()
    rows = lax.broadcasted_iota(I16, (HUBS, t), 0)
    ids = hub[...].astype(I16)
    count = onehot(rows == ids[0:1, :]) + onehot(rows == ids[1:2, :])
    hub_part = mm(count, msg).astype(BF)
    depth = h.shape[1]
    first = lax.rem(me[0], 2) == 0
    part_self = mm_tn(h[...], g[...]).astype(BF)
    part_neigh = mm_tn(a[...], g[...]).astype(BF)

    @pl.when(first)
    def _():
        mine[...] = hub_part
        send[0:depth, :] = part_self
        send[depth : 2 * depth, :] = part_neigh

    @pl.when(jnp.logical_not(first))
    def _():
        send[...] = hub_part
        mine[0:depth, :] = part_self
        mine[depth : 2 * depth, :] = part_neigh

    store.wait()
    loads[6].wait()
    loads[7].wait()


def spread_rows():
    row = lax.broadcasted_iota(I32, (GROUP * 16, 192), 0)
    col = lax.broadcasted_iota(I32, (GROUP * 16, 192), 1)
    chunk, s = row // 16, row % 16
    want = jnp.where(s < 8, (s // 2) * 32 + chunk * 2 + s % 2, 128 + (s - 8) * 16 + chunk)
    return onehot((s < 12) & (col == want))


def picks(places, at):
    return onehot((at == places[0]) | (at == places[1]) | (at == places[2]))


def pack_kernel(me, owner, slot, message, out):
    t = message.shape[0]
    n = out.shape[0]
    fan = slot.shape[0]
    device = lax.broadcasted_iota(I32, (n, t), 0)
    before = onehot(
        lax.broadcasted_iota(I16, (t, t), 0) < lax.broadcasted_iota(I16, (t, t), 1)
    )
    named = [device == owner[j] for j in range(fan)]
    hots = [onehot(f) for f in named]
    hot = jnp.concatenate(hots, axis=0)
    earlier = mm(hot, before)
    amount = jnp.sum(hot.astype(F32), axis=1, keepdims=True)
    base = jnp.zeros((n, 1), F32)
    ranks = []
    for j in range(fan):
        rank = jnp.where(named[j], earlier[j * n : (j + 1) * n, :] + base, 0.0)
        ranks.append(jnp.sum(rank, axis=0, keepdims=True).astype(I32))
        base = base + amount[j * n : (j + 1) * n, :]
    main, last = [], []
    for j, rank in enumerate(ranks):
        in_main = rank < MAIN
        main.append(jnp.where(in_main, owner[j] * MAIN + rank, -1).astype(I16))
        last.append(jnp.where(in_main, -1, owner[j] * REST + (rank - MAIN)).astype(I16))
    kinds = slot_kinds(me[0], slot[...], hots, ranks).astype(BF)

    msg = message[...]
    spread = spread_rows()
    rest = mm(picks(last, lax.broadcasted_iota(I16, (n * REST, t), 0)), msg).astype(BF)
    for g in range(n // GROUP):
        stacked = jnp.concatenate(
            [rest[g * 32 : (g + 1) * 32, q * 128 : (q + 1) * 128] for q in range(4)]
            + [kinds[g * GROUP : (g + 1) * GROUP, q * 128 : (q + 1) * 128] for q in range(4)],
            axis=0,
        )
        out[g * GROUP : (g + 1) * GROUP, 64:80, :] = (
            mm(spread, stacked).astype(BF).reshape(GROUP, 16, 128)
        )
    rows = mm(picks(main, lax.broadcasted_iota(I16, (n * MAIN, t), 0)), msg).astype(BF)
    for q in range(4):
        out[:, q * 16 : (q + 1) * 16, :] = rows[:, q * 128 : (q + 1) * 128].reshape(n, 16, 128)


def join_kernel(mine, got, held, out):
    for half in range(2):
        for q in range(2):
            at = half * 256 + q * 128
            total = mine[:, at : at + 128].astype(F32) + got[:, at : at + 128].astype(F32)
            first = FRONT + q * 16
            out[:, half, first : first + 16, :] = total.astype(BF).reshape(-1, 16, 128)


def reduce_kernel(received, out, kept, total, left):
    chips, each = received.shape[0], total.shape[0]
    acc = jnp.sum(received[:, :, FRONT : FRONT + 32, :].astype(F32), axis=0, keepdims=True)
    total[...] = jnp.broadcast_to(acc.astype(BF), total.shape)
    copies = [
        pltpu.make_async_copy(total, out.at[pl.ds(i * each, each)], left.at[1 + i])
        for i in range(chips // each)
    ]
    copies.append(
        pltpu.make_async_copy(received.at[:, :, pl.ds(0, FRONT), :], kept, left.at[0])
    )
    for copy in copies:
        copy.start()
    for copy in copies:
        copy.wait()


def front_kernel(received, g, ws, out, grad_self, rows, index):
    step = pl.program_id(0)
    n = received.shape[0]
    grad_self[...] = mm_nt(g[...], ws[...]).astype(BF)

    @pl.when(step == 0)
    def _():
        for q in range(4):
            rows[0 : n * MAIN, q * 128 : (q + 1) * 128] = received[
                :, q * 16 : (q + 1) * 16, :
            ].reshape(n * MAIN, 128)
        spread = spread_rows()
        main = []
        rest = [jnp.zeros((1, 128), F32), jnp.zeros((1, 128), F32)]
        for k in range(n // GROUP):
            tile = received[k * GROUP : (k + 1) * GROUP, 64:80, :].reshape(GROUP * 16, 128)
            stacked = mm_tn(spread, tile)
            for q in range(4):
                rows[n * MAIN + k * 32 : n * MAIN + (k + 1) * 32, q * 128 : (q + 1) * 128] = (
                    stacked[q * 32 : (q + 1) * 32, :].astype(BF)
                )
            main_slot = stacked[128:144, :] * 64.0 + stacked[144:160, :]
            rest_slot = stacked[160:176, :] * 64.0 + stacked[176:192, :]
            main.append(jnp.sum(main_slot[0:8, :], axis=0, keepdims=True))
            main.append(jnp.sum(main_slot[8:16, :], axis=0, keepdims=True))
            part = k * GROUP // 64
            rest[part] = rest[part] + jnp.sum(rest_slot, axis=0, keepdims=True)
        for g, line in enumerate(main + rest):
            index[g : g + 1, :] = line.astype(I32)

    block = out.shape[0]
    wanted = lax.broadcasted_iota(I32, (block, 128), 0) + step * block
    hot = jnp.concatenate(
        [onehot(wanted == index[g : g + 1, :]) for g in range(n * CAP // 128)], axis=1
    )
    out[...] = mm(hot, rows[...])


def fill_kernel(scale, mine, me, part, *refs):
    hub_grad, grad_w_self, grad_w_neigh, wide, done = refs[-5:]
    depth = grad_w_self.shape[0]
    hubs = (lax.rem(me[0], 2) == 0) == mine
    factor = jnp.where(hubs, 1.0, scale)
    steps = 4
    rows = HUBS // steps
    chips = rows // 16

    def copies(step):
        src = wide.at[pl.ds(step * rows, rows)]
        to_hubs = hub_grad.at[pl.ds(step * rows, rows)]
        weights = grad_w_self if step < steps // 2 else grad_w_neigh
        to_weights = weights.at[pl.ds(step * rows % depth, rows)]
        return (
            pltpu.make_async_copy(src, to_hubs, done.at[step]),
            pltpu.make_async_copy(src, to_weights, done.at[step]),
        )

    for step in range(steps):
        for half in range(2):
            for q in range(2):
                at = half * 256 + q * 128
                block = part[step * chips : (step + 1) * chips, half, q * 16 : (q + 1) * 16, :]
                wide[step * rows : (step + 1) * rows, at : at + 128] = (
                    block.reshape(rows, 128).astype(F32) * factor
                )
        to_hubs, to_weights = copies(step)
        pl.when(hubs)(to_hubs.start)
        pl.when(jnp.logical_not(hubs))(to_weights.start)
    for step in range(steps):
        to_hubs, to_weights = copies(step)
        pl.when(hubs)(to_hubs.wait)
        pl.when(jnp.logical_not(hubs))(to_weights.wait)


SMEM = pl.BlockSpec(memory_space=pltpu.SMEM)
HBM = pl.BlockSpec(memory_space=pltpu.HBM)
VMEM = pl.BlockSpec(memory_space=pltpu.VMEM)
PARAMS = pltpu.CompilerParams(vmem_limit_bytes=VMEM_LIMIT)


def in_hbm(x):
    return pltpu.with_memory_space_constraint(x, pltpu.HBM)


def in_vmem(x):
    return pltpu.with_memory_space_constraint(x, pltpu.VMEM)


def body(h_self, agg, grad_out, w_self, w_neigh, owner, slot, hub_refs):
    t, width = h_self.shape
    n = lax.axis_size("dev")
    me = lax.axis_index("dev").astype(I32).reshape(1)
    owner_t = owner.transpose(1, 2, 0)
    slot_t = slot.T
    hub_t = hub_refs.T
    swap = [(i, i ^ 1) for i in range(n)]

    with jax.named_scope("grads"):
        g, message, mine, send, owner_v, slot_v = pl.pallas_call(
            grads_kernel,
            out_shape=(
                pltpu.HBM((t, width), BF),
                pltpu.VMEM((t, width), BF),
                pltpu.VMEM((HUBS, width), BF),
                pltpu.VMEM((HUBS, width), BF),
                pltpu.VMEM(owner_t.shape, I32),
                pltpu.VMEM(slot_t.shape, I32),
            ),
            in_specs=[SMEM] + [HBM] * 8,
            out_specs=[HBM] + [VMEM] * 5,
            scratch_shapes=[pltpu.VMEM((t, width), BF)] * 3
            + [pltpu.VMEM((width, width), BF)] * 2
            + [
                pltpu.VMEM(hub_t.shape, I32),
                pltpu.VMEM((t, width), BF),
                pltpu.SemaphoreType.DMA((9,)),
            ],
            compiler_params=PARAMS,
        )(me, *map(in_hbm, (h_self, agg, grad_out, w_self, w_neigh, hub_t, owner_t, slot_t)))
    with jax.named_scope("core_exchange"):
        got = lax.ppermute(send, "dev", swap)
    with jax.named_scope("pack"):
        packed = pl.pallas_call(
            pack_kernel,
            out_shape=pltpu.VMEM((n, CHUNK, 128), BF),
            in_specs=[SMEM] + [VMEM] * 3,
            out_specs=VMEM,
            compiler_params=PARAMS,
        )(me, *map(in_vmem, (owner_v, slot_v, message)))
    with jax.named_scope("join"):
        packed = pl.pallas_call(
            join_kernel,
            out_shape=pltpu.VMEM((n // 2, 2, CHUNK, 128), BF),
            in_specs=[VMEM, VMEM, HBM],
            out_specs=VMEM,
            input_output_aliases={2: 0},
            compiler_params=PARAMS,
        )(in_vmem(mine), in_vmem(got), in_vmem(packed.reshape(n // 2, 2, CHUNK, 128)))
    with jax.named_scope("rows_to_owners"):
        received = lax.all_to_all(
            packed.reshape(n, CHUNK, 128), "dev", split_axis=0, concat_axis=0, tiled=True
        )
    with jax.named_scope("sum_parts"):
        total, kept = pl.pallas_call(
            reduce_kernel,
            out_shape=(
                pltpu.HBM((n // 2, 2, 32, 128), BF),
                pltpu.HBM((n // 2, 2, FRONT, 128), BF),
            ),
            in_specs=[VMEM],
            out_specs=[HBM] * 2,
            scratch_shapes=[
                pltpu.VMEM((8, 2, 32, 128), BF),
                pltpu.SemaphoreType.DMA((1 + n // 16,)),
            ],
            compiler_params=PARAMS,
        )(in_vmem(received.reshape(n // 2, 2, CHUNK, 128)))
        kept = kept.reshape(n, FRONT, 128)
    with jax.named_scope("sums_to_all"):
        own = lax.all_to_all(
            total.reshape(n, 32, 128), "dev", split_axis=0, concat_axis=0, tiled=True
        )
    with jax.named_scope("front"):
        front_grad, grad_self = pl.pallas_call(
            front_kernel,
            out_shape=(
                jax.ShapeDtypeStruct((OWN_DEV, width), F32),
                jax.ShapeDtypeStruct((t, width), BF),
            ),
            grid=(8,),
            in_specs=[
                pl.BlockSpec((n, FRONT, 128), lambda i: (0, 0, 0)),
                pl.BlockSpec((t // 8, width), lambda i: (i, 0)),
                pl.BlockSpec((width, width), lambda i: (0, 0)),
            ],
            out_specs=(
                pl.BlockSpec((OWN_DEV // 8, width), lambda i: (i, 0)),
                pl.BlockSpec((t // 8, width), lambda i: (i, 0)),
            ),
            scratch_shapes=[
                pltpu.VMEM((n * CAP, width), BF),
                pltpu.VMEM((24, 128), I32),
            ],
            compiler_params=PARAMS,
            cost_estimate=pl.CostEstimate(
                flops=2 * OWN_DEV * n * CAP * width, bytes_accessed=8 << 20, transcendentals=0
            ),
        )(in_hbm(kept), in_hbm(g), in_hbm(w_self))
    own, front_grad = lax.optimization_barrier((own, front_grad))
    with jax.named_scope("core_exchange_back"):
        other = lax.ppermute(own, "dev", swap)
    scale = 1.0 / (t * n) ** 0.5
    filled = ()
    for mine_too, part in ((True, own), (False, other)):
        with jax.named_scope("fill_own" if mine_too else "fill_other"):
            filled = pl.pallas_call(
                functools.partial(fill_kernel, scale, mine_too),
                out_shape=(
                    jax.ShapeDtypeStruct((HUBS, width), F32),
                    jax.ShapeDtypeStruct((width, width), F32),
                    jax.ShapeDtypeStruct((width, width), F32),
                ),
                in_specs=[SMEM, VMEM] + [HBM] * len(filled),
                out_specs=[HBM] * 3,
                scratch_shapes=[pltpu.VMEM((HUBS, width), F32), pltpu.SemaphoreType.DMA((4,))],
                input_output_aliases={2 + i: i for i in range(len(filled))},
                compiler_params=PARAMS,
                cost_estimate=pl.CostEstimate(
                    flops=HUBS * width, bytes_accessed=3 << 20, transcendentals=0
                ),
            )(me, part.reshape(n // 2, 2, 32, 128), *filled)
    hub_grad, grad_w_self, grad_w_neigh = filled
    return grad_self, front_grad, hub_grad, grad_w_self, grad_w_neigh


def solution(mesh):
    placed = (
        P("dev", None),
        P("dev", None),
        P("dev", None),
        P(),
        P(),
        P("dev", None, None),
        P("dev", None),
        P("dev", None),
    )
    return jax.shard_map(
        body,
        mesh=mesh,
        in_specs=placed,
        out_specs=(P("dev", None), P("dev", None), P(), P(), P()),
        check_vma=False,
    )
```

```python
import functools

import jax
import jax.numpy as jnp
from jax import lax
from jax.experimental import pallas as pl
from jax.experimental.pallas import tpu as pltpu
from jax.sharding import PartitionSpec as P

OWN_DEV = 2048
HUBS = 1024
FANOUT = 5
CAP = 18
MAIN = 16
REST = CAP - MAIN
FRONT = 80
CHUNK = 112
GROUP = 16
VMEM_LIMIT = 28 * 1024 * 1024
BF = jnp.bfloat16
F32 = jnp.float32
I32 = jnp.int32
I16 = jnp.int16


def mm(a, b):
    return jnp.dot(a, b, preferred_element_type=F32)


def mm_nt(a, b):
    return lax.dot_general(a, b, (((1,), (1,)), ((), ())), preferred_element_type=F32)


def mm_tn(a, b):
    return lax.dot_general(a, b, (((0,), (0,)), ((), ())), preferred_element_type=F32)


def onehot(flag):
    return jnp.where(flag, jnp.ones((), BF), jnp.zeros((), BF))


def slot_kinds(me, slot, hots, ranks):
    t = slot.shape[1]
    row = lax.broadcasted_iota(I32, (32, t), 0)
    values = []
    for j, rank in enumerate(ranks):
        value = slot[j : j + 1, :]
        at = row == rank
        high = jnp.where(at, (value // 64).astype(F32), 0.0)
        low = jnp.where(at, (value % 64).astype(F32), 0.0)
        values.append(jnp.concatenate([high, low], axis=0).astype(BF))
    by_rank = mm_nt(jnp.concatenate(hots, axis=1), jnp.concatenate(values, axis=1)).astype(BF)
    source = lax.broadcasted_iota(I32, (64, 512), 0)
    target = lax.broadcasted_iota(I32, (64, 512), 1)
    rank, part = source % 32, source // 32
    in_main = rank < MAIN
    lane = jnp.where(in_main, (me % 8) * MAIN + rank, (me % 64) * REST + rank - MAIN)
    kind = jnp.where(in_main, 0, 2) + part
    return mm(by_rank, onehot((rank < CAP) & (target == kind * 128 + lane)))


def hub_sums(message, hub):
    rows = lax.broadcasted_iota(I16, (HUBS, message.shape[0]), 0)
    ids = hub[...].astype(I16)
    count = onehot(rows == ids[0:1, :]) + onehot(rows == ids[1:2, :])
    return mm(count, message[...]).astype(BF)


def half_sums(hubs, message, hub, h, a, g, out):
    depth = h.shape[1]

    @pl.when(hubs)
    def _():
        out[...] = hub_sums(message, hub)

    @pl.when(jnp.logical_not(hubs))
    def _():
        out[0:depth, :] = mm_tn(h[...], g[...]).astype(BF)
        out[depth : 2 * depth, :] = mm_tn(a[...], g[...]).astype(BF)


def find_places(chip_row, owner, slot, places, kinds):
    fan, t = slot.shape
    n = kinds.shape[0]
    device = lax.broadcasted_iota(I32, (n, t), 0)
    before = onehot(
        lax.broadcasted_iota(I16, (t, t), 0) < lax.broadcasted_iota(I16, (t, t), 1)
    )
    named = [device == owner[j] for j in range(fan)]
    hots = [onehot(f) for f in named]
    hot = jnp.concatenate(hots, axis=0)
    earlier = mm(hot, before)
    amount = jnp.sum(hot.astype(F32), axis=1, keepdims=True)
    base = jnp.zeros((n, 1), F32)
    ranks = []
    for j in range(fan):
        rank = jnp.where(named[j], earlier[j * n : (j + 1) * n, :] + base, 0.0)
        ranks.append(jnp.sum(rank, axis=0, keepdims=True).astype(I32))
        base = base + amount[j * n : (j + 1) * n, :]
    for j, rank in enumerate(ranks):
        in_main = rank < MAIN
        places[j : j + 1, :] = jnp.where(in_main, owner[j] * MAIN + rank, -1)
        places[4 + j : 5 + j, :] = jnp.where(in_main, -1, owner[j] * REST + (rank - MAIN))
    kinds[...] = slot_kinds(chip_row, slot[...], hots, ranks).astype(BF)


def grads_kernel(
    me, h_in, a_in, go_in, ws_in, wn_in, hub_in, owner_in, slot_in,
    g_out, h, a, g, hub, message, send, places, kinds,
    go, ws, wn, owner, slot, arrived,
):
    loads = [
        pltpu.make_async_copy(src, dst, arrived.at[i])
        for i, (src, dst) in enumerate(
            (
                (owner_in, owner), (slot_in, slot),
                (h_in, h), (ws_in, ws), (a_in, a), (wn_in, wn), (go_in, go), (hub_in, hub),
            )
        )
    ]
    for load in loads:
        load.start()

    loads[0].wait()
    loads[1].wait()
    find_places(me[0], owner, slot, places, kinds)
    loads[2].wait()
    loads[3].wait()
    pre = mm(h[...], ws[...])
    loads[4].wait()
    loads[5].wait()
    pre = pre + mm(a[...], wn[...])
    loads[6].wait()
    sig = jax.nn.sigmoid(pre)
    g[...] = (go[...].astype(F32) * (sig * (1.0 + pre * (1.0 - sig)))).astype(BF)
    store = pltpu.make_async_copy(g, g_out, arrived.at[8])
    store.start()
    message[...] = (mm_nt(g[...], wn[...]) / FANOUT).astype(BF)
    loads[7].wait()
    half_sums(lax.rem(me[0], 2) == 1, message, hub, h, a, g, send)
    store.wait()


def spread_rows():
    row = lax.broadcasted_iota(I32, (GROUP * 16, 192), 0)
    col = lax.broadcasted_iota(I32, (GROUP * 16, 192), 1)
    chunk, s = row // 16, row % 16
    want = jnp.where(s < 8, (s // 2) * 32 + chunk * 2 + s % 2, 128 + (s - 8) * 16 + chunk)
    return onehot((s < 12) & (col == want))


def picks(places, at):
    return onehot((at == places[0]) | (at == places[1]) | (at == places[2]))


def pack_kernel(me, h, a, g, hub, message, places, kinds, out, mine):
    t = message.shape[0]
    n = out.shape[0]
    half_sums(lax.rem(me[0], 2) == 0, message, hub, h, a, g, mine)
    main = [places[j : j + 1, :].astype(I16) for j in range(3)]
    last = [places[4 + j : 5 + j, :].astype(I16) for j in range(3)]
    msg = message[...]
    spread = spread_rows()
    rest = mm(picks(last, lax.broadcasted_iota(I16, (n * REST, t), 0)), msg).astype(BF)
    for g in range(n // GROUP):
        stacked = jnp.concatenate(
            [rest[g * 32 : (g + 1) * 32, q * 128 : (q + 1) * 128] for q in range(4)]
            + [kinds[g * GROUP : (g + 1) * GROUP, q * 128 : (q + 1) * 128] for q in range(4)],
            axis=0,
        )
        out[g * GROUP : (g + 1) * GROUP, 64:80, :] = (
            mm(spread, stacked).astype(BF).reshape(GROUP, 16, 128)
        )
    rows = mm(picks(main, lax.broadcasted_iota(I16, (n * MAIN, t), 0)), msg).astype(BF)
    for q in range(4):
        out[:, q * 16 : (q + 1) * 16, :] = rows[:, q * 128 : (q + 1) * 128].reshape(n, 16, 128)


def join_kernel(mine, got, held, out):
    for half in range(2):
        for q in range(2):
            at = half * 256 + q * 128
            total = mine[:, at : at + 128].astype(F32) + got[:, at : at + 128].astype(F32)
            first = FRONT + q * 16
            out[:, half, first : first + 16, :] = total.astype(BF).reshape(-1, 16, 128)


def reduce_kernel(received, out, kept, total, left):
    chips, each = received.shape[0], total.shape[0]
    acc = jnp.sum(received[:, :, FRONT : FRONT + 32, :].astype(F32), axis=0, keepdims=True)
    total[...] = jnp.broadcast_to(acc.astype(BF), total.shape)
    copies = [
        pltpu.make_async_copy(total, out.at[pl.ds(i * each, each)], left.at[1 + i])
        for i in range(chips // each)
    ]
    copies.append(
        pltpu.make_async_copy(received.at[:, :, pl.ds(0, FRONT), :], kept, left.at[0])
    )
    for copy in copies:
        copy.start()
    for copy in copies:
        copy.wait()


def front_kernel(received, g, ws, out, grad_self, rows, index):
    step = pl.program_id(0)
    n = received.shape[0]
    grad_self[...] = mm_nt(g[...], ws[...]).astype(BF)

    @pl.when(step == 0)
    def _():
        for q in range(4):
            rows[0 : n * MAIN, q * 128 : (q + 1) * 128] = received[
                :, q * 16 : (q + 1) * 16, :
            ].reshape(n * MAIN, 128)
        spread = spread_rows()
        main = []
        rest = [jnp.zeros((1, 128), F32), jnp.zeros((1, 128), F32)]
        for k in range(n // GROUP):
            tile = received[k * GROUP : (k + 1) * GROUP, 64:80, :].reshape(GROUP * 16, 128)
            stacked = mm_tn(spread, tile)
            for q in range(4):
                rows[n * MAIN + k * 32 : n * MAIN + (k + 1) * 32, q * 128 : (q + 1) * 128] = (
                    stacked[q * 32 : (q + 1) * 32, :].astype(BF)
                )
            main_slot = stacked[128:144, :] * 64.0 + stacked[144:160, :]
            rest_slot = stacked[160:176, :] * 64.0 + stacked[176:192, :]
            main.append(jnp.sum(main_slot[0:8, :], axis=0, keepdims=True))
            main.append(jnp.sum(main_slot[8:16, :], axis=0, keepdims=True))
            part = k * GROUP // 64
            rest[part] = rest[part] + jnp.sum(rest_slot, axis=0, keepdims=True)
        for g, line in enumerate(main + rest):
            index[g : g + 1, :] = line.astype(I32)

    block = out.shape[0]
    wanted = lax.broadcasted_iota(I32, (block, 128), 0) + step * block
    hot = jnp.concatenate(
        [onehot(wanted == index[g : g + 1, :]) for g in range(n * CAP // 128)], axis=1
    )
    out[...] = mm(hot, rows[...])


def fill_kernel(scale, mine, me, part, *refs):
    hub_grad, grad_w_self, grad_w_neigh, wide, done = refs[-5:]
    depth = grad_w_self.shape[0]
    hubs = (lax.rem(me[0], 2) == 0) == mine
    factor = jnp.where(hubs, 1.0, scale)
    steps = 4
    rows = HUBS // steps
    chips = rows // 16

    def copies(step):
        src = wide.at[pl.ds(step * rows, rows)]
        to_hubs = hub_grad.at[pl.ds(step * rows, rows)]
        weights = grad_w_self if step < steps // 2 else grad_w_neigh
        to_weights = weights.at[pl.ds(step * rows % depth, rows)]
        return (
            pltpu.make_async_copy(src, to_hubs, done.at[step]),
            pltpu.make_async_copy(src, to_weights, done.at[step]),
        )

    for step in range(steps):
        for half in range(2):
            for q in range(2):
                at = half * 256 + q * 128
                block = part[step * chips : (step + 1) * chips, half, q * 16 : (q + 1) * 16, :]
                wide[step * rows : (step + 1) * rows, at : at + 128] = (
                    block.reshape(rows, 128).astype(F32) * factor
                )
        to_hubs, to_weights = copies(step)
        pl.when(hubs)(to_hubs.start)
        pl.when(jnp.logical_not(hubs))(to_weights.start)
    for step in range(steps):
        to_hubs, to_weights = copies(step)
        pl.when(hubs)(to_hubs.wait)
        pl.when(jnp.logical_not(hubs))(to_weights.wait)


SMEM = pl.BlockSpec(memory_space=pltpu.SMEM)
HBM = pl.BlockSpec(memory_space=pltpu.HBM)
VMEM = pl.BlockSpec(memory_space=pltpu.VMEM)
PARAMS = pltpu.CompilerParams(vmem_limit_bytes=VMEM_LIMIT)


def in_hbm(x):
    return pltpu.with_memory_space_constraint(x, pltpu.HBM)


def in_vmem(x):
    return pltpu.with_memory_space_constraint(x, pltpu.VMEM)


def body(h_self, agg, grad_out, w_self, w_neigh, owner, slot, hub_refs):
    t, width = h_self.shape
    n = lax.axis_size("dev")
    me = lax.axis_index("dev").astype(I32).reshape(1)
    owner_t = owner.transpose(1, 2, 0)
    slot_t = slot.T
    hub_t = hub_refs.T
    swap = [(i, i ^ 1) for i in range(n)]

    with jax.named_scope("grads"):
        g_kept, h, a, g, hub, message, send, places, kinds = pl.pallas_call(
            grads_kernel,
            out_shape=(
                pltpu.HBM((t, width), BF),
                pltpu.VMEM((t, width), BF),
                pltpu.VMEM((t, width), BF),
                pltpu.VMEM((t, width), BF),
                pltpu.VMEM(hub_t.shape, I32),
                pltpu.VMEM((t, width), BF),
                pltpu.VMEM((HUBS, width), BF),
                pltpu.VMEM((8, t), I32),
                pltpu.VMEM((n, 512), BF),
            ),
            in_specs=[SMEM] + [HBM] * 8,
            out_specs=[HBM] + [VMEM] * 8,
            scratch_shapes=[
                pltpu.VMEM((t, width), BF),
                pltpu.VMEM((width, width), BF),
                pltpu.VMEM((width, width), BF),
                pltpu.VMEM(owner_t.shape, I32),
                pltpu.VMEM(slot_t.shape, I32),
                pltpu.SemaphoreType.DMA((9,)),
            ],
            compiler_params=PARAMS,
        )(me, *map(in_hbm, (h_self, agg, grad_out, w_self, w_neigh, hub_t, owner_t, slot_t)))
    with jax.named_scope("core_exchange"):
        got = lax.ppermute(send, "dev", swap)
    with jax.named_scope("pack"):
        packed, mine = pl.pallas_call(
            pack_kernel,
            out_shape=(pltpu.VMEM((n, CHUNK, 128), BF), pltpu.VMEM((HUBS, width), BF)),
            in_specs=[SMEM] + [VMEM] * 7,
            out_specs=[VMEM] * 2,
            compiler_params=PARAMS,
        )(me, *map(in_vmem, (h, a, g, hub, message, places, kinds)))
    with jax.named_scope("join"):
        packed = pl.pallas_call(
            join_kernel,
            out_shape=pltpu.VMEM((n // 2, 2, CHUNK, 128), BF),
            in_specs=[VMEM, VMEM, HBM],
            out_specs=VMEM,
            input_output_aliases={2: 0},
            compiler_params=PARAMS,
        )(in_vmem(mine), in_vmem(got), in_vmem(packed.reshape(n // 2, 2, CHUNK, 128)))
    with jax.named_scope("rows_to_owners"):
        received = lax.all_to_all(
            packed.reshape(n, CHUNK, 128), "dev", split_axis=0, concat_axis=0, tiled=True
        )
    with jax.named_scope("sum_parts"):
        total, kept = pl.pallas_call(
            reduce_kernel,
            out_shape=(
                pltpu.HBM((n // 2, 2, 32, 128), BF),
                pltpu.HBM((n // 2, 2, FRONT, 128), BF),
            ),
            in_specs=[VMEM],
            out_specs=[HBM] * 2,
            scratch_shapes=[
                pltpu.VMEM((8, 2, 32, 128), BF),
                pltpu.SemaphoreType.DMA((1 + n // 16,)),
            ],
            compiler_params=PARAMS,
        )(in_vmem(received.reshape(n // 2, 2, CHUNK, 128)))
        kept = kept.reshape(n, FRONT, 128)
    with jax.named_scope("sums_to_all"):
        own = lax.all_to_all(
            total.reshape(n, 32, 128), "dev", split_axis=0, concat_axis=0, tiled=True
        )
    with jax.named_scope("front"):
        front_grad, grad_self = pl.pallas_call(
            front_kernel,
            out_shape=(
                jax.ShapeDtypeStruct((OWN_DEV, width), F32),
                jax.ShapeDtypeStruct((t, width), BF),
            ),
            grid=(8,),
            in_specs=[
                pl.BlockSpec((n, FRONT, 128), lambda i: (0, 0, 0)),
                pl.BlockSpec((t // 8, width), lambda i: (i, 0)),
                pl.BlockSpec((width, width), lambda i: (0, 0)),
            ],
            out_specs=(
                pl.BlockSpec((OWN_DEV // 8, width), lambda i: (i, 0)),
                pl.BlockSpec((t // 8, width), lambda i: (i, 0)),
            ),
            scratch_shapes=[
                pltpu.VMEM((n * CAP, width), BF),
                pltpu.VMEM((24, 128), I32),
            ],
            compiler_params=PARAMS,
            cost_estimate=pl.CostEstimate(
                flops=2 * OWN_DEV * n * CAP * width, bytes_accessed=8 << 20, transcendentals=0
            ),
        )(in_hbm(kept), in_hbm(g_kept), in_hbm(w_self))
    own, front_grad = lax.optimization_barrier((own, front_grad))
    with jax.named_scope("core_exchange_back"):
        other = lax.ppermute(own, "dev", swap)
    scale = 1.0 / (t * n) ** 0.5
    filled = ()
    for mine_too, part in ((True, own), (False, other)):
        with jax.named_scope("fill_own" if mine_too else "fill_other"):
            filled = pl.pallas_call(
                functools.partial(fill_kernel, scale, mine_too),
                out_shape=(
                    jax.ShapeDtypeStruct((HUBS, width), F32),
                    jax.ShapeDtypeStruct((width, width), F32),
                    jax.ShapeDtypeStruct((width, width), F32),
                ),
                in_specs=[SMEM, VMEM] + [HBM] * len(filled),
                out_specs=[HBM] * 3,
                scratch_shapes=[pltpu.VMEM((HUBS, width), F32), pltpu.SemaphoreType.DMA((4,))],
                input_output_aliases={2 + i: i for i in range(len(filled))},
                compiler_params=PARAMS,
                cost_estimate=pl.CostEstimate(
                    flops=HUBS * width, bytes_accessed=3 << 20, transcendentals=0
                ),
            )(me, part.reshape(n // 2, 2, 32, 128), *filled)
    hub_grad, grad_w_self, grad_w_neigh = filled
    return grad_self, front_grad, hub_grad, grad_w_self, grad_w_neigh


def solution(mesh):
    placed = (
        P("dev", None),
        P("dev", None),
        P("dev", None),
        P(),
        P(),
        P("dev", None, None),
        P("dev", None),
        P("dev", None),
    )
    return jax.shard_map(
        body,
        mesh=mesh,
        in_specs=placed,
        out_specs=(P("dev", None), P("dev", None), P(), P(), P()),
        check_vma=False,
    )
```

```python
import functools

import jax
import jax.numpy as jnp
from jax import lax
from jax.experimental import pallas as pl
from jax.experimental.pallas import tpu as pltpu
from jax.sharding import PartitionSpec as P

OWN_DEV = 2048
HUBS = 1024
FANOUT = 5
CAP = 18
MAIN = 16
REST = CAP - MAIN
FRONT = 80
CHUNK = 112
GROUP = 16
VMEM_LIMIT = 28 * 1024 * 1024
BF = jnp.bfloat16
F32 = jnp.float32
I32 = jnp.int32
I16 = jnp.int16


def mm(a, b):
    return jnp.dot(a, b, preferred_element_type=F32)


def mm_nt(a, b):
    return lax.dot_general(a, b, (((1,), (1,)), ((), ())), preferred_element_type=F32)


def mm_tn(a, b):
    return lax.dot_general(a, b, (((0,), (0,)), ((), ())), preferred_element_type=F32)


def onehot(flag):
    return jnp.where(flag, jnp.ones((), BF), jnp.zeros((), BF))


def slot_kinds(me, slot, hots, ranks):
    t = slot.shape[1]
    row = lax.broadcasted_iota(I32, (32, t), 0)
    values = []
    for j, rank in enumerate(ranks):
        value = slot[j : j + 1, :]
        at = row == rank
        high = jnp.where(at, (value // 64).astype(F32), 0.0)
        low = jnp.where(at, (value % 64).astype(F32), 0.0)
        values.append(jnp.concatenate([high, low], axis=0).astype(BF))
    by_rank = mm_nt(jnp.concatenate(hots, axis=1), jnp.concatenate(values, axis=1)).astype(BF)
    source = lax.broadcasted_iota(I32, (64, 512), 0)
    target = lax.broadcasted_iota(I32, (64, 512), 1)
    rank, part = source % 32, source // 32
    in_main = rank < MAIN
    lane = jnp.where(in_main, (me % 8) * MAIN + rank, (me % 64) * REST + rank - MAIN)
    kind = jnp.where(in_main, 0, 2) + part
    return mm(by_rank, onehot((rank < CAP) & (target == kind * 128 + lane)))


def hub_sums(message, hub):
    rows = lax.broadcasted_iota(I16, (HUBS, message.shape[0]), 0)
    ids = hub[...].astype(I16)
    count = onehot(rows == ids[0:1, :]) + onehot(rows == ids[1:2, :])
    return mm(count, message[...]).astype(BF)


def half_sums(hubs, message, hub, h, a, g, out):
    depth = h.shape[1]

    @pl.when(hubs)
    def _():
        out[...] = hub_sums(message, hub)

    @pl.when(jnp.logical_not(hubs))
    def _():
        out[0:depth, :] = mm_tn(h[...], g[...]).astype(BF)
        out[depth : 2 * depth, :] = mm_tn(a[...], g[...]).astype(BF)


def find_places(chip_row, owner, slot, places, kinds):
    fan, t = slot.shape
    n = kinds.shape[0]
    device = lax.broadcasted_iota(I32, (n, t), 0)
    before = onehot(
        lax.broadcasted_iota(I16, (t, t), 0) < lax.broadcasted_iota(I16, (t, t), 1)
    )
    named = [device == owner[j] for j in range(fan)]
    hots = [onehot(f) for f in named]
    hot = jnp.concatenate(hots, axis=0)
    earlier = mm(hot, before)
    amount = jnp.sum(hot.astype(F32), axis=1, keepdims=True)
    base = jnp.zeros((n, 1), F32)
    ranks = []
    for j in range(fan):
        rank = jnp.where(named[j], earlier[j * n : (j + 1) * n, :] + base, 0.0)
        ranks.append(jnp.sum(rank, axis=0, keepdims=True).astype(I32))
        base = base + amount[j * n : (j + 1) * n, :]
    for j, rank in enumerate(ranks):
        in_main = rank < MAIN
        places[j : j + 1, :] = jnp.where(in_main, owner[j] * MAIN + rank, -1)
        places[4 + j : 5 + j, :] = jnp.where(in_main, -1, owner[j] * REST + (rank - MAIN))
    kinds[...] = slot_kinds(chip_row, slot[...], hots, ranks).astype(BF)


def grads_kernel(
    me, h_in, a_in, go_in, ws_in, wn_in, hub_in, owner_in, slot_in,
    g_out, h, a, g, hub, message, send, places, kinds,
    go, ws, wn, owner, slot, arrived,
):
    loads = [
        pltpu.make_async_copy(src, dst, arrived.at[i])
        for i, (src, dst) in enumerate(
            (
                (owner_in, owner), (slot_in, slot),
                (h_in, h), (ws_in, ws), (a_in, a), (wn_in, wn), (go_in, go), (hub_in, hub),
            )
        )
    ]
    for load in loads:
        load.start()

    loads[0].wait()
    loads[1].wait()
    find_places(me[0], owner, slot, places, kinds)
    loads[2].wait()
    loads[3].wait()
    pre = mm(h[...], ws[...])
    loads[4].wait()
    loads[5].wait()
    pre = pre + mm(a[...], wn[...])
    loads[6].wait()
    sig = jax.nn.sigmoid(pre)
    g[...] = (go[...].astype(F32) * (sig * (1.0 + pre * (1.0 - sig)))).astype(BF)
    store = pltpu.make_async_copy(g, g_out, arrived.at[8])
    store.start()
    message[...] = (mm_nt(g[...], wn[...]) / FANOUT).astype(BF)
    loads[7].wait()
    half_sums(lax.rem(me[0], 2) == 1, message, hub, h, a, g, send)
    store.wait()


def spread_rows():
    row = lax.broadcasted_iota(I32, (GROUP * 16, 192), 0)
    col = lax.broadcasted_iota(I32, (GROUP * 16, 192), 1)
    chunk, s = row // 16, row % 16
    want = jnp.where(s < 8, (s // 2) * 32 + chunk * 2 + s % 2, 128 + (s - 8) * 16 + chunk)
    return onehot((s < 12) & (col == want))


def picks(places, at):
    return onehot((at == places[0]) | (at == places[1]) | (at == places[2]))


def pack_kernel(me, h, a, g, hub, message, places, kinds, out, mine):
    t = message.shape[0]
    n = out.shape[0]
    half_sums(lax.rem(me[0], 2) == 0, message, hub, h, a, g, mine)
    main = [places[j : j + 1, :].astype(I16) for j in range(3)]
    last = [places[4 + j : 5 + j, :].astype(I16) for j in range(3)]
    msg = message[...]
    spread = spread_rows()
    rest = mm(picks(last, lax.broadcasted_iota(I16, (n * REST, t), 0)), msg).astype(BF)
    for g in range(n // GROUP):
        stacked = jnp.concatenate(
            [rest[g * 32 : (g + 1) * 32, q * 128 : (q + 1) * 128] for q in range(4)]
            + [kinds[g * GROUP : (g + 1) * GROUP, q * 128 : (q + 1) * 128] for q in range(4)],
            axis=0,
        )
        out[g * GROUP : (g + 1) * GROUP, 64:80, :] = (
            mm(spread, stacked).astype(BF).reshape(GROUP, 16, 128)
        )
    rows = mm(picks(main, lax.broadcasted_iota(I16, (n * MAIN, t), 0)), msg).astype(BF)
    for q in range(4):
        out[:, q * 16 : (q + 1) * 16, :] = rows[:, q * 128 : (q + 1) * 128].reshape(n, 16, 128)


def join_kernel(mine, got, held, out):
    for half in range(2):
        for q in range(2):
            at = half * 256 + q * 128
            total = mine[:, at : at + 128].astype(F32) + got[:, at : at + 128].astype(F32)
            first = FRONT + q * 16
            out[:, half, first : first + 16, :] = total.astype(BF).reshape(-1, 16, 128)


def reduce_kernel(received, out, kept, total, left):
    chips, each = received.shape[0], total.shape[0]
    rows = pltpu.make_async_copy(received.at[:, :, pl.ds(0, FRONT), :], kept, left.at[0])
    rows.start()
    acc = jnp.sum(received[:, :, FRONT : FRONT + 32, :].astype(F32), axis=0, keepdims=True)
    total[...] = jnp.broadcast_to(acc.astype(BF), total.shape)
    copies = [
        pltpu.make_async_copy(total, out.at[pl.ds(i * each, each)], left.at[1 + i])
        for i in range(chips // each)
    ]
    for copy in copies:
        copy.start()
    for copy in copies:
        copy.wait()
    rows.wait()


def front_kernel(received, g, ws, out, grad_self, rows, index):
    step = pl.program_id(0)
    n = received.shape[0]
    grad_self[...] = mm_nt(g[...], ws[...]).astype(BF)

    @pl.when(step == 0)
    def _():
        for q in range(4):
            rows[0 : n * MAIN, q * 128 : (q + 1) * 128] = received[
                :, q * 16 : (q + 1) * 16, :
            ].reshape(n * MAIN, 128)
        spread = spread_rows()
        main = []
        rest = [jnp.zeros((1, 128), F32), jnp.zeros((1, 128), F32)]
        for k in range(n // GROUP):
            tile = received[k * GROUP : (k + 1) * GROUP, 64:80, :].reshape(GROUP * 16, 128)
            stacked = mm_tn(spread, tile)
            for q in range(4):
                rows[n * MAIN + k * 32 : n * MAIN + (k + 1) * 32, q * 128 : (q + 1) * 128] = (
                    stacked[q * 32 : (q + 1) * 32, :].astype(BF)
                )
            main_slot = stacked[128:144, :] * 64.0 + stacked[144:160, :]
            rest_slot = stacked[160:176, :] * 64.0 + stacked[176:192, :]
            main.append(jnp.sum(main_slot[0:8, :], axis=0, keepdims=True))
            main.append(jnp.sum(main_slot[8:16, :], axis=0, keepdims=True))
            part = k * GROUP // 64
            rest[part] = rest[part] + jnp.sum(rest_slot, axis=0, keepdims=True)
        for g, line in enumerate(main + rest):
            index[g : g + 1, :] = line.astype(I32)

    block = out.shape[0]
    wanted = lax.broadcasted_iota(I32, (block, 128), 0) + step * block
    hot = jnp.concatenate(
        [onehot(wanted == index[g : g + 1, :]) for g in range(n * CAP // 128)], axis=1
    )
    out[...] = mm(hot, rows[...])


def fill_kernel(scale, mine, me, part, *refs):
    hub_grad, grad_w_self, grad_w_neigh, wide, done = refs[-5:]
    depth = grad_w_self.shape[0]
    hubs = (lax.rem(me[0], 2) == 0) == mine
    factor = jnp.where(hubs, 1.0, scale)
    steps = 4
    rows = HUBS // steps
    chips = rows // 16

    def copies(step):
        src = wide.at[pl.ds(step * rows, rows)]
        to_hubs = hub_grad.at[pl.ds(step * rows, rows)]
        weights = grad_w_self if step < steps // 2 else grad_w_neigh
        to_weights = weights.at[pl.ds(step * rows % depth, rows)]
        return (
            pltpu.make_async_copy(src, to_hubs, done.at[step]),
            pltpu.make_async_copy(src, to_weights, done.at[step]),
        )

    for step in range(steps):
        for half in range(2):
            for q in range(2):
                at = half * 256 + q * 128
                block = part[step * chips : (step + 1) * chips, half, q * 16 : (q + 1) * 16, :]
                wide[step * rows : (step + 1) * rows, at : at + 128] = (
                    block.reshape(rows, 128).astype(F32) * factor
                )
        to_hubs, to_weights = copies(step)
        pl.when(hubs)(to_hubs.start)
        pl.when(jnp.logical_not(hubs))(to_weights.start)
    for step in range(steps):
        to_hubs, to_weights = copies(step)
        pl.when(hubs)(to_hubs.wait)
        pl.when(jnp.logical_not(hubs))(to_weights.wait)


SMEM = pl.BlockSpec(memory_space=pltpu.SMEM)
HBM = pl.BlockSpec(memory_space=pltpu.HBM)
VMEM = pl.BlockSpec(memory_space=pltpu.VMEM)
PARAMS = pltpu.CompilerParams(vmem_limit_bytes=VMEM_LIMIT)


def in_hbm(x):
    return pltpu.with_memory_space_constraint(x, pltpu.HBM)


def in_vmem(x):
    return pltpu.with_memory_space_constraint(x, pltpu.VMEM)


def body(h_self, agg, grad_out, w_self, w_neigh, owner, slot, hub_refs):
    t, width = h_self.shape
    n = lax.axis_size("dev")
    me = lax.axis_index("dev").astype(I32).reshape(1)
    owner_t = owner.transpose(1, 2, 0)
    slot_t = slot.T
    hub_t = hub_refs.T
    swap = [(i, i ^ 1) for i in range(n)]

    with jax.named_scope("grads"):
        g_kept, h, a, g, hub, message, send, places, kinds = pl.pallas_call(
            grads_kernel,
            out_shape=(
                pltpu.HBM((t, width), BF),
                pltpu.VMEM((t, width), BF),
                pltpu.VMEM((t, width), BF),
                pltpu.VMEM((t, width), BF),
                pltpu.VMEM(hub_t.shape, I32),
                pltpu.VMEM((t, width), BF),
                pltpu.VMEM((HUBS, width), BF),
                pltpu.VMEM((8, t), I32),
                pltpu.VMEM((n, 512), BF),
            ),
            in_specs=[SMEM] + [HBM] * 8,
            out_specs=[HBM] + [VMEM] * 8,
            scratch_shapes=[
                pltpu.VMEM((t, width), BF),
                pltpu.VMEM((width, width), BF),
                pltpu.VMEM((width, width), BF),
                pltpu.VMEM(owner_t.shape, I32),
                pltpu.VMEM(slot_t.shape, I32),
                pltpu.SemaphoreType.DMA((9,)),
            ],
            compiler_params=PARAMS,
        )(me, *map(in_hbm, (h_self, agg, grad_out, w_self, w_neigh, hub_t, owner_t, slot_t)))
    with jax.named_scope("core_exchange"):
        got = lax.ppermute(send, "dev", swap)
    with jax.named_scope("pack"):
        packed, mine = pl.pallas_call(
            pack_kernel,
            out_shape=(pltpu.VMEM((n, CHUNK, 128), BF), pltpu.VMEM((HUBS, width), BF)),
            in_specs=[SMEM] + [VMEM] * 7,
            out_specs=[VMEM] * 2,
            compiler_params=PARAMS,
        )(me, *map(in_vmem, (h, a, g, hub, message, places, kinds)))
    with jax.named_scope("join"):
        packed = pl.pallas_call(
            join_kernel,
            out_shape=pltpu.VMEM((n // 2, 2, CHUNK, 128), BF),
            in_specs=[VMEM, VMEM, HBM],
            out_specs=VMEM,
            input_output_aliases={2: 0},
            compiler_params=PARAMS,
        )(in_vmem(mine), in_vmem(got), in_vmem(packed.reshape(n // 2, 2, CHUNK, 128)))
    with jax.named_scope("rows_to_owners"):
        received = lax.all_to_all(
            packed.reshape(n, CHUNK, 128), "dev", split_axis=0, concat_axis=0, tiled=True
        )
    with jax.named_scope("sum_parts"):
        total, kept = pl.pallas_call(
            reduce_kernel,
            out_shape=(
                pltpu.HBM((n // 2, 2, 32, 128), BF),
                pltpu.HBM((n // 2, 2, FRONT, 128), BF),
            ),
            in_specs=[VMEM],
            out_specs=[HBM] * 2,
            scratch_shapes=[
                pltpu.VMEM((8, 2, 32, 128), BF),
                pltpu.SemaphoreType.DMA((1 + n // 16,)),
            ],
            compiler_params=PARAMS,
        )(in_vmem(received.reshape(n // 2, 2, CHUNK, 128)))
        kept = kept.reshape(n, FRONT, 128)
    with jax.named_scope("sums_to_all"):
        own = lax.all_to_all(
            total.reshape(n, 32, 128), "dev", split_axis=0, concat_axis=0, tiled=True
        )
    with jax.named_scope("front"):
        front_grad, grad_self = pl.pallas_call(
            front_kernel,
            out_shape=(
                jax.ShapeDtypeStruct((OWN_DEV, width), F32),
                jax.ShapeDtypeStruct((t, width), BF),
            ),
            grid=(8,),
            in_specs=[
                pl.BlockSpec((n, FRONT, 128), lambda i: (0, 0, 0)),
                pl.BlockSpec((t // 8, width), lambda i: (i, 0)),
                pl.BlockSpec((width, width), lambda i: (0, 0)),
            ],
            out_specs=(
                pl.BlockSpec((OWN_DEV // 8, width), lambda i: (i, 0)),
                pl.BlockSpec((t // 8, width), lambda i: (i, 0)),
            ),
            scratch_shapes=[
                pltpu.VMEM((n * CAP, width), BF),
                pltpu.VMEM((24, 128), I32),
            ],
            compiler_params=PARAMS,
            cost_estimate=pl.CostEstimate(
                flops=2 * OWN_DEV * n * CAP * width, bytes_accessed=8 << 20, transcendentals=0
            ),
        )(in_hbm(kept), in_hbm(g_kept), in_hbm(w_self))
    own, front_grad = lax.optimization_barrier((own, front_grad))
    with jax.named_scope("core_exchange_back"):
        other = lax.ppermute(own, "dev", swap)
    scale = 1.0 / (t * n) ** 0.5
    filled = ()
    for mine_too, part in ((True, own), (False, other)):
        with jax.named_scope("fill_own" if mine_too else "fill_other"):
            filled = pl.pallas_call(
                functools.partial(fill_kernel, scale, mine_too),
                out_shape=(
                    jax.ShapeDtypeStruct((HUBS, width), F32),
                    jax.ShapeDtypeStruct((width, width), F32),
                    jax.ShapeDtypeStruct((width, width), F32),
                ),
                in_specs=[SMEM, VMEM] + [HBM] * len(filled),
                out_specs=[HBM] * 3,
                scratch_shapes=[pltpu.VMEM((HUBS, width), F32), pltpu.SemaphoreType.DMA((4,))],
                input_output_aliases={2 + i: i for i in range(len(filled))},
                compiler_params=PARAMS,
                cost_estimate=pl.CostEstimate(
                    flops=HUBS * width, bytes_accessed=3 << 20, transcendentals=0
                ),
            )(me, part.reshape(n // 2, 2, 32, 128), *filled)
    hub_grad, grad_w_self, grad_w_neigh = filled
    return grad_self, front_grad, hub_grad, grad_w_self, grad_w_neigh


def solution(mesh):
    placed = (
        P("dev", None),
        P("dev", None),
        P("dev", None),
        P(),
        P(),
        P("dev", None, None),
        P("dev", None),
        P("dev", None),
    )
    return jax.shard_map(
        body,
        mesh=mesh,
        in_specs=placed,
        out_specs=(P("dev", None), P("dev", None), P(), P(), P()),
        check_vma=False,
    )
```

```python
import functools

import jax
import jax.numpy as jnp
from jax import lax
from jax.experimental import pallas as pl
from jax.experimental.pallas import tpu as pltpu
from jax.sharding import PartitionSpec as P

OWN_DEV = 2048
HUBS = 1024
FANOUT = 5
CAP = 18
MAIN = 16
REST = CAP - MAIN
FRONT = 80
CHUNK = 112
GROUP = 16
VMEM_LIMIT = 28 * 1024 * 1024
BF = jnp.bfloat16
F32 = jnp.float32
I32 = jnp.int32
I16 = jnp.int16


def mm(a, b):
    return jnp.dot(a, b, preferred_element_type=F32)


def mm_nt(a, b):
    return lax.dot_general(a, b, (((1,), (1,)), ((), ())), preferred_element_type=F32)


def mm_tn(a, b):
    return lax.dot_general(a, b, (((0,), (0,)), ((), ())), preferred_element_type=F32)


def onehot(flag):
    return jnp.where(flag, jnp.ones((), BF), jnp.zeros((), BF))


def slot_kinds(me, slot, hots, ranks):
    t = slot.shape[1]
    row = lax.broadcasted_iota(I32, (32, t), 0)
    values = []
    for j, rank in enumerate(ranks):
        value = slot[j : j + 1, :]
        at = row == rank
        high = jnp.where(at, (value // 64).astype(F32), 0.0)
        low = jnp.where(at, (value % 64).astype(F32), 0.0)
        values.append(jnp.concatenate([high, low], axis=0).astype(BF))
    by_rank = mm_nt(jnp.concatenate(hots, axis=1), jnp.concatenate(values, axis=1)).astype(BF)
    source = lax.broadcasted_iota(I32, (64, 512), 0)
    target = lax.broadcasted_iota(I32, (64, 512), 1)
    rank, part = source % 32, source // 32
    in_main = rank < MAIN
    lane = jnp.where(in_main, (me % 8) * MAIN + rank, (me % 64) * REST + rank - MAIN)
    kind = jnp.where(in_main, 0, 2) + part
    return mm(by_rank, onehot((rank < CAP) & (target == kind * 128 + lane)))


def hub_sums(message, hub):
    rows = lax.broadcasted_iota(I16, (HUBS, message.shape[0]), 0)
    ids = hub[...].astype(I16)
    count = onehot(rows == ids[0:1, :]) + onehot(rows == ids[1:2, :])
    return mm(count, message[...]).astype(BF)


def half_sums(hubs, message, hub, h, a, g, out):
    depth = h.shape[1]

    @pl.when(hubs)
    def _():
        out[...] = hub_sums(message, hub)

    @pl.when(jnp.logical_not(hubs))
    def _():
        out[0:depth, :] = mm_tn(h[...], g[...]).astype(BF)
        out[depth : 2 * depth, :] = mm_tn(a[...], g[...]).astype(BF)


def find_places(chip_row, owner, slot, places, kinds):
    fan, t = slot.shape
    n = kinds.shape[0]
    device = lax.broadcasted_iota(I32, (n, t), 0)
    before = onehot(
        lax.broadcasted_iota(I16, (t, t), 0) < lax.broadcasted_iota(I16, (t, t), 1)
    )
    named = [device == owner[j] for j in range(fan)]
    hots = [onehot(f) for f in named]
    hot = jnp.concatenate(hots, axis=0)
    earlier = mm(hot, before)
    amount = jnp.sum(hot.astype(F32), axis=1, keepdims=True)
    base = jnp.zeros((n, 1), F32)
    ranks = []
    for j in range(fan):
        rank = jnp.where(named[j], earlier[j * n : (j + 1) * n, :] + base, 0.0)
        ranks.append(jnp.sum(rank, axis=0, keepdims=True).astype(I32))
        base = base + amount[j * n : (j + 1) * n, :]
    for j, rank in enumerate(ranks):
        in_main = rank < MAIN
        places[j : j + 1, :] = jnp.where(in_main, owner[j] * MAIN + rank, -1)
        places[4 + j : 5 + j, :] = jnp.where(in_main, -1, owner[j] * REST + (rank - MAIN))
    kinds[...] = slot_kinds(chip_row, slot[...], hots, ranks).astype(BF)


def grads_kernel(
    me, h_in, a_in, go_in, ws_in, wn_in, hub_in, owner_in, slot_in,
    g_out, h, a, g, hub, message, send, places, kinds,
    go, ws, wn, owner, slot, arrived,
):
    loads = [
        pltpu.make_async_copy(src, dst, arrived.at[i])
        for i, (src, dst) in enumerate(
            (
                (owner_in, owner), (slot_in, slot),
                (h_in, h), (ws_in, ws), (a_in, a), (wn_in, wn), (go_in, go), (hub_in, hub),
            )
        )
    ]
    for load in loads:
        load.start()

    loads[0].wait()
    loads[1].wait()
    find_places(me[0], owner, slot, places, kinds)
    loads[2].wait()
    loads[3].wait()
    pre = mm(h[...], ws[...])
    loads[4].wait()
    loads[5].wait()
    pre = pre + mm(a[...], wn[...])
    loads[6].wait()
    sig = jax.nn.sigmoid(pre)
    g[...] = (go[...].astype(F32) * (sig * (1.0 + pre * (1.0 - sig)))).astype(BF)
    store = pltpu.make_async_copy(g, g_out, arrived.at[8])
    store.start()
    message[...] = (mm_nt(g[...], wn[...]) / FANOUT).astype(BF)
    loads[7].wait()
    half_sums(lax.rem(me[0], 2) == 1, message, hub, h, a, g, send)
    store.wait()


def spread_rows():
    row = lax.broadcasted_iota(I32, (GROUP * 16, 192), 0)
    col = lax.broadcasted_iota(I32, (GROUP * 16, 192), 1)
    chunk, s = row // 16, row % 16
    want = jnp.where(s < 8, (s // 2) * 32 + chunk * 2 + s % 2, 128 + (s - 8) * 16 + chunk)
    return onehot((s < 12) & (col == want))


def picks(places, at):
    return onehot((at == places[0]) | (at == places[1]) | (at == places[2]))


def pack_kernel(me, h, a, g, hub, message, places, kinds, out, mine):
    t = message.shape[0]
    n = out.shape[0]
    half_sums(lax.rem(me[0], 2) == 0, message, hub, h, a, g, mine)
    main = [places[j : j + 1, :].astype(I16) for j in range(3)]
    last = [places[4 + j : 5 + j, :].astype(I16) for j in range(3)]
    msg = message[...]
    spread = spread_rows()
    rest = mm(picks(last, lax.broadcasted_iota(I16, (n * REST, t), 0)), msg).astype(BF)
    stacked = jnp.concatenate(
        [
            jnp.concatenate(
                [rest[k * 32 : (k + 1) * 32, q * 128 : (q + 1) * 128] for q in range(4)]
                + [kinds[k * GROUP : (k + 1) * GROUP, q * 128 : (q + 1) * 128] for q in range(4)],
                axis=0,
            )
            for k in range(n // GROUP)
        ],
        axis=1,
    )
    tiles = mm(spread, stacked).astype(BF)
    for k in range(n // GROUP):
        out[k * GROUP : (k + 1) * GROUP, 64:80, :] = tiles[:, k * 128 : (k + 1) * 128].reshape(
            GROUP, 16, 128
        )
    rows = mm(picks(main, lax.broadcasted_iota(I16, (n * MAIN, t), 0)), msg).astype(BF)
    for q in range(4):
        out[:, q * 16 : (q + 1) * 16, :] = rows[:, q * 128 : (q + 1) * 128].reshape(n, 16, 128)


def join_kernel(mine, got, held, out):
    for half in range(2):
        for q in range(2):
            at = half * 256 + q * 128
            total = mine[:, at : at + 128].astype(F32) + got[:, at : at + 128].astype(F32)
            first = FRONT + q * 16
            out[:, half, first : first + 16, :] = total.astype(BF).reshape(-1, 16, 128)


def reduce_kernel(received, out, kept, total, left):
    chips, each = received.shape[0], total.shape[0]
    rows = pltpu.make_async_copy(received.at[:, :, pl.ds(0, FRONT), :], kept, left.at[0])
    rows.start()
    acc = jnp.sum(received[:, :, FRONT : FRONT + 32, :].astype(F32), axis=0, keepdims=True)
    total[...] = jnp.broadcast_to(acc.astype(BF), total.shape)
    copies = [
        pltpu.make_async_copy(total, out.at[pl.ds(i * each, each)], left.at[1 + i])
        for i in range(chips // each)
    ]
    for copy in copies:
        copy.start()
    for copy in copies:
        copy.wait()
    rows.wait()


def front_kernel(received, g, ws, out, grad_self, rows, index):
    step = pl.program_id(0)
    n = received.shape[0]
    grad_self[...] = mm_nt(g[...], ws[...]).astype(BF)

    @pl.when(step == 0)
    def _():
        for q in range(4):
            rows[0 : n * MAIN, q * 128 : (q + 1) * 128] = received[
                :, q * 16 : (q + 1) * 16, :
            ].reshape(n * MAIN, 128)
        spread = spread_rows()
        main = []
        rest = [jnp.zeros((1, 128), F32), jnp.zeros((1, 128), F32)]
        for k in range(n // GROUP):
            tile = received[k * GROUP : (k + 1) * GROUP, 64:80, :].reshape(GROUP * 16, 128)
            stacked = mm_tn(spread, tile)
            for q in range(4):
                rows[n * MAIN + k * 32 : n * MAIN + (k + 1) * 32, q * 128 : (q + 1) * 128] = (
                    stacked[q * 32 : (q + 1) * 32, :].astype(BF)
                )
            main_slot = stacked[128:144, :] * 64.0 + stacked[144:160, :]
            rest_slot = stacked[160:176, :] * 64.0 + stacked[176:192, :]
            main.append(jnp.sum(main_slot[0:8, :], axis=0, keepdims=True))
            main.append(jnp.sum(main_slot[8:16, :], axis=0, keepdims=True))
            part = k * GROUP // 64
            rest[part] = rest[part] + jnp.sum(rest_slot, axis=0, keepdims=True)
        for g, line in enumerate(main + rest):
            index[g : g + 1, :] = line.astype(I32)

    block = out.shape[0]
    wanted = lax.broadcasted_iota(I32, (block, 128), 0) + step * block
    hot = jnp.concatenate(
        [onehot(wanted == index[g : g + 1, :]) for g in range(n * CAP // 128)], axis=1
    )
    out[...] = mm(hot, rows[...])


def fill_kernel(scale, mine, me, part, *refs):
    hub_grad, grad_w_self, grad_w_neigh, wide, done = refs[-5:]
    depth = grad_w_self.shape[0]
    hubs = (lax.rem(me[0], 2) == 0) == mine
    factor = jnp.where(hubs, 1.0, scale)
    steps = 4
    rows = HUBS // steps
    chips = rows // 16

    def copies(step):
        src = wide.at[pl.ds(step * rows, rows)]
        to_hubs = hub_grad.at[pl.ds(step * rows, rows)]
        weights = grad_w_self if step < steps // 2 else grad_w_neigh
        to_weights = weights.at[pl.ds(step * rows % depth, rows)]
        return (
            pltpu.make_async_copy(src, to_hubs, done.at[step]),
            pltpu.make_async_copy(src, to_weights, done.at[step]),
        )

    for step in range(steps):
        for half in range(2):
            for q in range(2):
                at = half * 256 + q * 128
                block = part[step * chips : (step + 1) * chips, half, q * 16 : (q + 1) * 16, :]
                wide[step * rows : (step + 1) * rows, at : at + 128] = (
                    block.reshape(rows, 128).astype(F32) * factor
                )
        to_hubs, to_weights = copies(step)
        pl.when(hubs)(to_hubs.start)
        pl.when(jnp.logical_not(hubs))(to_weights.start)
    for step in range(steps):
        to_hubs, to_weights = copies(step)
        pl.when(hubs)(to_hubs.wait)
        pl.when(jnp.logical_not(hubs))(to_weights.wait)


SMEM = pl.BlockSpec(memory_space=pltpu.SMEM)
HBM = pl.BlockSpec(memory_space=pltpu.HBM)
VMEM = pl.BlockSpec(memory_space=pltpu.VMEM)
PARAMS = pltpu.CompilerParams(vmem_limit_bytes=VMEM_LIMIT)


def in_hbm(x):
    return pltpu.with_memory_space_constraint(x, pltpu.HBM)


def in_vmem(x):
    return pltpu.with_memory_space_constraint(x, pltpu.VMEM)


def body(h_self, agg, grad_out, w_self, w_neigh, owner, slot, hub_refs):
    t, width = h_self.shape
    n = lax.axis_size("dev")
    me = lax.axis_index("dev").astype(I32).reshape(1)
    owner_t = owner.transpose(1, 2, 0)
    slot_t = slot.T
    hub_t = hub_refs.T
    swap = [(i, i ^ 1) for i in range(n)]

    with jax.named_scope("grads"):
        g_kept, h, a, g, hub, message, send, places, kinds = pl.pallas_call(
            grads_kernel,
            out_shape=(
                pltpu.HBM((t, width), BF),
                pltpu.VMEM((t, width), BF),
                pltpu.VMEM((t, width), BF),
                pltpu.VMEM((t, width), BF),
                pltpu.VMEM(hub_t.shape, I32),
                pltpu.VMEM((t, width), BF),
                pltpu.VMEM((HUBS, width), BF),
                pltpu.VMEM((8, t), I32),
                pltpu.VMEM((n, 512), BF),
            ),
            in_specs=[SMEM] + [HBM] * 8,
            out_specs=[HBM] + [VMEM] * 8,
            scratch_shapes=[
                pltpu.VMEM((t, width), BF),
                pltpu.VMEM((width, width), BF),
                pltpu.VMEM((width, width), BF),
                pltpu.VMEM(owner_t.shape, I32),
                pltpu.VMEM(slot_t.shape, I32),
                pltpu.SemaphoreType.DMA((9,)),
            ],
            compiler_params=PARAMS,
        )(me, *map(in_hbm, (h_self, agg, grad_out, w_self, w_neigh, hub_t, owner_t, slot_t)))
    with jax.named_scope("core_exchange"):
        got = lax.ppermute(send, "dev", swap)
    with jax.named_scope("pack"):
        packed, mine = pl.pallas_call(
            pack_kernel,
            out_shape=(pltpu.VMEM((n, CHUNK, 128), BF), pltpu.VMEM((HUBS, width), BF)),
            in_specs=[SMEM] + [VMEM] * 7,
            out_specs=[VMEM] * 2,
            compiler_params=PARAMS,
        )(me, *map(in_vmem, (h, a, g, hub, message, places, kinds)))
    with jax.named_scope("join"):
        packed = pl.pallas_call(
            join_kernel,
            out_shape=pltpu.VMEM((n // 2, 2, CHUNK, 128), BF),
            in_specs=[VMEM, VMEM, HBM],
            out_specs=VMEM,
            input_output_aliases={2: 0},
            compiler_params=PARAMS,
        )(in_vmem(mine), in_vmem(got), in_vmem(packed.reshape(n // 2, 2, CHUNK, 128)))
    with jax.named_scope("rows_to_owners"):
        received = lax.all_to_all(
            packed.reshape(n, CHUNK, 128), "dev", split_axis=0, concat_axis=0, tiled=True
        )
    with jax.named_scope("sum_parts"):
        total, kept = pl.pallas_call(
            reduce_kernel,
            out_shape=(
                pltpu.HBM((n // 2, 2, 32, 128), BF),
                pltpu.HBM((n // 2, 2, FRONT, 128), BF),
            ),
            in_specs=[VMEM],
            out_specs=[HBM] * 2,
            scratch_shapes=[
                pltpu.VMEM((8, 2, 32, 128), BF),
                pltpu.SemaphoreType.DMA((1 + n // 16,)),
            ],
            compiler_params=PARAMS,
        )(in_vmem(received.reshape(n // 2, 2, CHUNK, 128)))
        kept = kept.reshape(n, FRONT, 128)
    with jax.named_scope("sums_to_all"):
        own = lax.all_to_all(
            total.reshape(n, 32, 128), "dev", split_axis=0, concat_axis=0, tiled=True
        )
    with jax.named_scope("front"):
        front_grad, grad_self = pl.pallas_call(
            front_kernel,
            out_shape=(
                jax.ShapeDtypeStruct((OWN_DEV, width), F32),
                jax.ShapeDtypeStruct((t, width), BF),
            ),
            grid=(8,),
            in_specs=[
                pl.BlockSpec((n, FRONT, 128), lambda i: (0, 0, 0)),
                pl.BlockSpec((t // 8, width), lambda i: (i, 0)),
                pl.BlockSpec((width, width), lambda i: (0, 0)),
            ],
            out_specs=(
                pl.BlockSpec((OWN_DEV // 8, width), lambda i: (i, 0)),
                pl.BlockSpec((t // 8, width), lambda i: (i, 0)),
            ),
            scratch_shapes=[
                pltpu.VMEM((n * CAP, width), BF),
                pltpu.VMEM((24, 128), I32),
            ],
            compiler_params=PARAMS,
            cost_estimate=pl.CostEstimate(
                flops=2 * OWN_DEV * n * CAP * width, bytes_accessed=8 << 20, transcendentals=0
            ),
        )(in_hbm(kept), in_hbm(g_kept), in_hbm(w_self))
    own, front_grad = lax.optimization_barrier((own, front_grad))
    with jax.named_scope("core_exchange_back"):
        other = lax.ppermute(own, "dev", swap)
    scale = 1.0 / (t * n) ** 0.5
    filled = ()
    for mine_too, part in ((True, own), (False, other)):
        with jax.named_scope("fill_own" if mine_too else "fill_other"):
            filled = pl.pallas_call(
                functools.partial(fill_kernel, scale, mine_too),
                out_shape=(
                    jax.ShapeDtypeStruct((HUBS, width), F32),
                    jax.ShapeDtypeStruct((width, width), F32),
                    jax.ShapeDtypeStruct((width, width), F32),
                ),
                in_specs=[SMEM, VMEM] + [HBM] * len(filled),
                out_specs=[HBM] * 3,
                scratch_shapes=[pltpu.VMEM((HUBS, width), F32), pltpu.SemaphoreType.DMA((4,))],
                input_output_aliases={2 + i: i for i in range(len(filled))},
                compiler_params=PARAMS,
                cost_estimate=pl.CostEstimate(
                    flops=HUBS * width, bytes_accessed=3 << 20, transcendentals=0
                ),
            )(me, part.reshape(n // 2, 2, 32, 128), *filled)
    hub_grad, grad_w_self, grad_w_neigh = filled
    return grad_self, front_grad, hub_grad, grad_w_self, grad_w_neigh


def solution(mesh):
    placed = (
        P("dev", None),
        P("dev", None),
        P("dev", None),
        P(),
        P(),
        P("dev", None, None),
        P("dev", None),
        P("dev", None),
    )
    return jax.shard_map(
        body,
        mesh=mesh,
        in_specs=placed,
        out_specs=(P("dev", None), P("dev", None), P(), P(), P()),
        check_vma=False,
    )
```

```python
import functools

import jax
import jax.numpy as jnp
from jax import lax
from jax.experimental import pallas as pl
from jax.experimental.pallas import tpu as pltpu
from jax.sharding import PartitionSpec as P

OWN_DEV = 2048
HUBS = 1024
FANOUT = 5
CAP = 18
MAIN = 16
REST = CAP - MAIN
FRONT = 80
CHUNK = 112
GROUP = 16
VMEM_LIMIT = 28 * 1024 * 1024
BF = jnp.bfloat16
F32 = jnp.float32
I32 = jnp.int32
I16 = jnp.int16


def mm(a, b):
    return jnp.dot(a, b, preferred_element_type=F32)


def mm_nt(a, b):
    return lax.dot_general(a, b, (((1,), (1,)), ((), ())), preferred_element_type=F32)


def mm_tn(a, b):
    return lax.dot_general(a, b, (((0,), (0,)), ((), ())), preferred_element_type=F32)


def onehot(flag):
    return jnp.where(flag, jnp.ones((), BF), jnp.zeros((), BF))


def slot_kinds(me, slot, hots, ranks):
    t = slot.shape[1]
    row = lax.broadcasted_iota(I32, (32, t), 0)
    values = []
    for j, rank in enumerate(ranks):
        value = slot[j : j + 1, :]
        at = row == rank
        high = jnp.where(at, (value // 64).astype(F32), 0.0)
        low = jnp.where(at, (value % 64).astype(F32), 0.0)
        values.append(jnp.concatenate([high, low], axis=0).astype(BF))
    by_rank = mm_nt(jnp.concatenate(hots, axis=1), jnp.concatenate(values, axis=1)).astype(BF)
    source = lax.broadcasted_iota(I32, (64, 512), 0)
    target = lax.broadcasted_iota(I32, (64, 512), 1)
    rank, part = source % 32, source // 32
    in_main = rank < MAIN
    lane = jnp.where(in_main, (me % 8) * MAIN + rank, (me % 64) * REST + rank - MAIN)
    kind = jnp.where(in_main, 0, 2) + part
    return mm(by_rank, onehot((rank < CAP) & (target == kind * 128 + lane)))


def hub_sums(message, hub):
    rows = lax.broadcasted_iota(I16, (HUBS, message.shape[0]), 0)
    ids = hub[...].astype(I16)
    count = onehot(rows == ids[0:1, :]) + onehot(rows == ids[1:2, :])
    return mm(count, message[...]).astype(BF)


def half_sums(hubs, message, hub, h, a, g, out):
    depth = h.shape[1]

    @pl.when(hubs)
    def _():
        out[...] = hub_sums(message, hub)

    @pl.when(jnp.logical_not(hubs))
    def _():
        out[0:depth, :] = mm_tn(h[...], g[...]).astype(BF)
        out[depth : 2 * depth, :] = mm_tn(a[...], g[...]).astype(BF)


def find_places(chip_row, owner, slot, places, kinds):
    fan, t = slot.shape
    n = kinds.shape[0]
    device = lax.broadcasted_iota(I32, (n, t), 0)
    before = onehot(
        lax.broadcasted_iota(I16, (t, t), 0) < lax.broadcasted_iota(I16, (t, t), 1)
    )
    named = [device == owner[j] for j in range(fan)]
    hots = [onehot(f) for f in named]
    hot = jnp.concatenate(hots, axis=0)
    earlier = mm(hot, before)
    amount = jnp.sum(hot.astype(F32), axis=1, keepdims=True)
    base = jnp.zeros((n, 1), F32)
    ranks = []
    for j in range(fan):
        rank = jnp.where(named[j], earlier[j * n : (j + 1) * n, :] + base, 0.0)
        ranks.append(jnp.sum(rank, axis=0, keepdims=True).astype(I32))
        base = base + amount[j * n : (j + 1) * n, :]
    for j, rank in enumerate(ranks):
        in_main = rank < MAIN
        places[j : j + 1, :] = jnp.where(in_main, owner[j] * MAIN + rank, -1)
        places[4 + j : 5 + j, :] = jnp.where(in_main, -1, owner[j] * REST + (rank - MAIN))
    kinds[...] = slot_kinds(chip_row, slot[...], hots, ranks).astype(BF)


def grads_kernel(
    me, h_in, a_in, go_in, ws_in, wn_in, hub_in, owner_in, slot_in,
    h, a, g, hub, message, send, places, kinds,
    go, ws, wn, owner, slot, arrived,
):
    loads = [
        pltpu.make_async_copy(src, dst, arrived.at[i])
        for i, (src, dst) in enumerate(
            (
                (owner_in, owner), (slot_in, slot),
                (h_in, h), (ws_in, ws), (a_in, a), (wn_in, wn), (go_in, go), (hub_in, hub),
            )
        )
    ]
    for load in loads:
        load.start()

    loads[0].wait()
    loads[1].wait()
    find_places(me[0], owner, slot, places, kinds)
    loads[2].wait()
    loads[3].wait()
    pre = mm(h[...], ws[...])
    loads[4].wait()
    loads[5].wait()
    pre = pre + mm(a[...], wn[...])
    loads[6].wait()
    sig = jax.nn.sigmoid(pre)
    g[...] = (go[...].astype(F32) * (sig * (1.0 + pre * (1.0 - sig)))).astype(BF)
    message[...] = (mm_nt(g[...], wn[...]) / FANOUT).astype(BF)
    loads[7].wait()
    half_sums(lax.rem(me[0], 2) == 1, message, hub, h, a, g, send)


def spread_rows():
    row = lax.broadcasted_iota(I32, (GROUP * 16, 192), 0)
    col = lax.broadcasted_iota(I32, (GROUP * 16, 192), 1)
    chunk, s = row // 16, row % 16
    want = jnp.where(s < 8, (s // 2) * 32 + chunk * 2 + s % 2, 128 + (s - 8) * 16 + chunk)
    return onehot((s < 12) & (col == want))


def picks(places, at):
    return onehot((at == places[0]) | (at == places[1]) | (at == places[2]))


def pack_kernel(me, h, a, g, hub, message, places, kinds, out, mine, g_out, stored):
    store = pltpu.make_async_copy(g, g_out, stored)
    store.start()
    t = message.shape[0]
    n = out.shape[0]
    half_sums(lax.rem(me[0], 2) == 0, message, hub, h, a, g, mine)
    main = [places[j : j + 1, :].astype(I16) for j in range(3)]
    last = [places[4 + j : 5 + j, :].astype(I16) for j in range(3)]
    msg = message[...]
    spread = spread_rows()
    rest = mm(picks(last, lax.broadcasted_iota(I16, (n * REST, t), 0)), msg).astype(BF)
    stacked = jnp.concatenate(
        [
            jnp.concatenate(
                [rest[k * 32 : (k + 1) * 32, q * 128 : (q + 1) * 128] for q in range(4)]
                + [kinds[k * GROUP : (k + 1) * GROUP, q * 128 : (q + 1) * 128] for q in range(4)],
                axis=0,
            )
            for k in range(n // GROUP)
        ],
        axis=1,
    )
    tiles = mm(spread, stacked).astype(BF)
    for k in range(n // GROUP):
        out[k * GROUP : (k + 1) * GROUP, 64:80, :] = tiles[:, k * 128 : (k + 1) * 128].reshape(
            GROUP, 16, 128
        )
    rows = mm(picks(main, lax.broadcasted_iota(I16, (n * MAIN, t), 0)), msg).astype(BF)
    for q in range(4):
        out[:, q * 16 : (q + 1) * 16, :] = rows[:, q * 128 : (q + 1) * 128].reshape(n, 16, 128)
    store.wait()


def join_kernel(mine, got, held, out):
    for half in range(2):
        for q in range(2):
            at = half * 256 + q * 128
            total = mine[:, at : at + 128].astype(F32) + got[:, at : at + 128].astype(F32)
            first = FRONT + q * 16
            out[:, half, first : first + 16, :] = total.astype(BF).reshape(-1, 16, 128)


def reduce_kernel(received, out, kept, total, left):
    chips, each = received.shape[0], total.shape[0]
    rows = pltpu.make_async_copy(received.at[:, :, pl.ds(0, FRONT), :], kept, left.at[0])
    rows.start()
    acc = jnp.sum(received[:, :, FRONT : FRONT + 32, :].astype(F32), axis=0, keepdims=True)
    total[...] = jnp.broadcast_to(acc.astype(BF), total.shape)
    copies = [
        pltpu.make_async_copy(total, out.at[pl.ds(i * each, each)], left.at[1 + i])
        for i in range(chips // each)
    ]
    for copy in copies:
        copy.start()
    for copy in copies:
        copy.wait()
    rows.wait()


def front_kernel(received, g, ws, out, grad_self, rows, index):
    step = pl.program_id(0)
    n = received.shape[0]
    grad_self[...] = mm_nt(g[...], ws[...]).astype(BF)

    @pl.when(step == 0)
    def _():
        for q in range(4):
            rows[0 : n * MAIN, q * 128 : (q + 1) * 128] = received[
                :, q * 16 : (q + 1) * 16, :
            ].reshape(n * MAIN, 128)
        spread = spread_rows()
        main = []
        rest = [jnp.zeros((1, 128), F32), jnp.zeros((1, 128), F32)]
        for k in range(n // GROUP):
            tile = received[k * GROUP : (k + 1) * GROUP, 64:80, :].reshape(GROUP * 16, 128)
            stacked = mm_tn(spread, tile)
            for q in range(4):
                rows[n * MAIN + k * 32 : n * MAIN + (k + 1) * 32, q * 128 : (q + 1) * 128] = (
                    stacked[q * 32 : (q + 1) * 32, :].astype(BF)
                )
            main_slot = stacked[128:144, :] * 64.0 + stacked[144:160, :]
            rest_slot = stacked[160:176, :] * 64.0 + stacked[176:192, :]
            main.append(jnp.sum(main_slot[0:8, :], axis=0, keepdims=True))
            main.append(jnp.sum(main_slot[8:16, :], axis=0, keepdims=True))
            part = k * GROUP // 64
            rest[part] = rest[part] + jnp.sum(rest_slot, axis=0, keepdims=True)
        for g, line in enumerate(main + rest):
            index[g : g + 1, :] = line.astype(I32)

    block = out.shape[0]
    wanted = lax.broadcasted_iota(I32, (block, 128), 0) + step * block
    hot = jnp.concatenate(
        [onehot(wanted == index[g : g + 1, :]) for g in range(n * CAP // 128)], axis=1
    )
    out[...] = mm(hot, rows[...])


def fill_kernel(scale, mine, me, part, *refs):
    hub_grad, grad_w_self, grad_w_neigh, wide, done = refs[-5:]
    depth = grad_w_self.shape[0]
    hubs = (lax.rem(me[0], 2) == 0) == mine
    factor = jnp.where(hubs, 1.0, scale)
    steps = 4
    rows = HUBS // steps
    chips = rows // 16

    def copies(step):
        src = wide.at[pl.ds(step * rows, rows)]
        to_hubs = hub_grad.at[pl.ds(step * rows, rows)]
        weights = grad_w_self if step < steps // 2 else grad_w_neigh
        to_weights = weights.at[pl.ds(step * rows % depth, rows)]
        return (
            pltpu.make_async_copy(src, to_hubs, done.at[step]),
            pltpu.make_async_copy(src, to_weights, done.at[step]),
        )

    for step in range(steps):
        for half in range(2):
            for q in range(2):
                at = half * 256 + q * 128
                block = part[step * chips : (step + 1) * chips, half, q * 16 : (q + 1) * 16, :]
                wide[step * rows : (step + 1) * rows, at : at + 128] = (
                    block.reshape(rows, 128).astype(F32) * factor
                )
        to_hubs, to_weights = copies(step)
        pl.when(hubs)(to_hubs.start)
        pl.when(jnp.logical_not(hubs))(to_weights.start)
    for step in range(steps):
        to_hubs, to_weights = copies(step)
        pl.when(hubs)(to_hubs.wait)
        pl.when(jnp.logical_not(hubs))(to_weights.wait)


SMEM = pl.BlockSpec(memory_space=pltpu.SMEM)
HBM = pl.BlockSpec(memory_space=pltpu.HBM)
VMEM = pl.BlockSpec(memory_space=pltpu.VMEM)
PARAMS = pltpu.CompilerParams(vmem_limit_bytes=VMEM_LIMIT)


def in_hbm(x):
    return pltpu.with_memory_space_constraint(x, pltpu.HBM)


def in_vmem(x):
    return pltpu.with_memory_space_constraint(x, pltpu.VMEM)


def body(h_self, agg, grad_out, w_self, w_neigh, owner, slot, hub_refs):
    t, width = h_self.shape
    n = lax.axis_size("dev")
    me = lax.axis_index("dev").astype(I32).reshape(1)
    owner_t = owner.transpose(1, 2, 0)
    slot_t = slot.T
    hub_t = hub_refs.T
    swap = [(i, i ^ 1) for i in range(n)]

    with jax.named_scope("grads"):
        h, a, g, hub, message, send, places, kinds = pl.pallas_call(
            grads_kernel,
            out_shape=(
                pltpu.VMEM((t, width), BF),
                pltpu.VMEM((t, width), BF),
                pltpu.VMEM((t, width), BF),
                pltpu.VMEM(hub_t.shape, I32),
                pltpu.VMEM((t, width), BF),
                pltpu.VMEM((HUBS, width), BF),
                pltpu.VMEM((8, t), I32),
                pltpu.VMEM((n, 512), BF),
            ),
            in_specs=[SMEM] + [HBM] * 8,
            out_specs=[VMEM] * 8,
            scratch_shapes=[
                pltpu.VMEM((t, width), BF),
                pltpu.VMEM((width, width), BF),
                pltpu.VMEM((width, width), BF),
                pltpu.VMEM(owner_t.shape, I32),
                pltpu.VMEM(slot_t.shape, I32),
                pltpu.SemaphoreType.DMA((8,)),
            ],
            compiler_params=PARAMS,
        )(me, *map(in_hbm, (h_self, agg, grad_out, w_self, w_neigh, hub_t, owner_t, slot_t)))
    with jax.named_scope("core_exchange"):
        got = lax.ppermute(send, "dev", swap)
    with jax.named_scope("pack"):
        packed, mine, g_kept = pl.pallas_call(
            pack_kernel,
            out_shape=(
                pltpu.VMEM((n, CHUNK, 128), BF),
                pltpu.VMEM((HUBS, width), BF),
                pltpu.HBM((t, width), BF),
            ),
            in_specs=[SMEM] + [VMEM] * 7,
            out_specs=[VMEM] * 2 + [HBM],
            scratch_shapes=[pltpu.SemaphoreType.DMA],
            compiler_params=PARAMS,
        )(me, *map(in_vmem, (h, a, g, hub, message, places, kinds)))
    with jax.named_scope("join"):
        packed = pl.pallas_call(
            join_kernel,
            out_shape=pltpu.VMEM((n // 2, 2, CHUNK, 128), BF),
            in_specs=[VMEM, VMEM, HBM],
            out_specs=VMEM,
            input_output_aliases={2: 0},
            compiler_params=PARAMS,
        )(in_vmem(mine), in_vmem(got), in_vmem(packed.reshape(n // 2, 2, CHUNK, 128)))
    with jax.named_scope("rows_to_owners"):
        received = lax.all_to_all(
            packed.reshape(n, CHUNK, 128), "dev", split_axis=0, concat_axis=0, tiled=True
        )
    with jax.named_scope("sum_parts"):
        total, kept = pl.pallas_call(
            reduce_kernel,
            out_shape=(
                pltpu.HBM((n // 2, 2, 32, 128), BF),
                pltpu.HBM((n // 2, 2, FRONT, 128), BF),
            ),
            in_specs=[VMEM],
            out_specs=[HBM] * 2,
            scratch_shapes=[
                pltpu.VMEM((8, 2, 32, 128), BF),
                pltpu.SemaphoreType.DMA((1 + n // 16,)),
            ],
            compiler_params=PARAMS,
        )(in_vmem(received.reshape(n // 2, 2, CHUNK, 128)))
        kept = kept.reshape(n, FRONT, 128)
    with jax.named_scope("sums_to_all"):
        own = lax.all_to_all(
            total.reshape(n, 32, 128), "dev", split_axis=0, concat_axis=0, tiled=True
        )
    with jax.named_scope("front"):
        front_grad, grad_self = pl.pallas_call(
            front_kernel,
            out_shape=(
                jax.ShapeDtypeStruct((OWN_DEV, width), F32),
                jax.ShapeDtypeStruct((t, width), BF),
            ),
            grid=(8,),
            in_specs=[
                pl.BlockSpec((n, FRONT, 128), lambda i: (0, 0, 0)),
                pl.BlockSpec((t // 8, width), lambda i: (i, 0)),
                pl.BlockSpec((width, width), lambda i: (0, 0)),
            ],
            out_specs=(
                pl.BlockSpec((OWN_DEV // 8, width), lambda i: (i, 0)),
                pl.BlockSpec((t // 8, width), lambda i: (i, 0)),
            ),
            scratch_shapes=[
                pltpu.VMEM((n * CAP, width), BF),
                pltpu.VMEM((24, 128), I32),
            ],
            compiler_params=PARAMS,
            cost_estimate=pl.CostEstimate(
                flops=2 * OWN_DEV * n * CAP * width, bytes_accessed=8 << 20, transcendentals=0
            ),
        )(in_hbm(kept), in_hbm(g_kept), in_hbm(w_self))
    own, front_grad = lax.optimization_barrier((own, front_grad))
    with jax.named_scope("core_exchange_back"):
        other = lax.ppermute(own, "dev", swap)
    scale = 1.0 / (t * n) ** 0.5
    filled = ()
    for mine_too, part in ((True, own), (False, other)):
        with jax.named_scope("fill_own" if mine_too else "fill_other"):
            filled = pl.pallas_call(
                functools.partial(fill_kernel, scale, mine_too),
                out_shape=(
                    jax.ShapeDtypeStruct((HUBS, width), F32),
                    jax.ShapeDtypeStruct((width, width), F32),
                    jax.ShapeDtypeStruct((width, width), F32),
                ),
                in_specs=[SMEM, VMEM] + [HBM] * len(filled),
                out_specs=[HBM] * 3,
                scratch_shapes=[pltpu.VMEM((HUBS, width), F32), pltpu.SemaphoreType.DMA((4,))],
                input_output_aliases={2 + i: i for i in range(len(filled))},
                compiler_params=PARAMS,
                cost_estimate=pl.CostEstimate(
                    flops=HUBS * width, bytes_accessed=3 << 20, transcendentals=0
                ),
            )(me, part.reshape(n // 2, 2, 32, 128), *filled)
    hub_grad, grad_w_self, grad_w_neigh = filled
    return grad_self, front_grad, hub_grad, grad_w_self, grad_w_neigh


def solution(mesh):
    placed = (
        P("dev", None),
        P("dev", None),
        P("dev", None),
        P(),
        P(),
        P("dev", None, None),
        P("dev", None),
        P("dev", None),
    )
    return jax.shard_map(
        body,
        mesh=mesh,
        in_specs=placed,
        out_specs=(P("dev", None), P("dev", None), P(), P(), P()),
        check_vma=False,
    )
```

```python
import functools

import jax
import jax.numpy as jnp
from jax import lax
from jax.experimental import pallas as pl
from jax.experimental.pallas import tpu as pltpu
from jax.sharding import PartitionSpec as P

OWN_DEV = 2048
HUBS = 1024
FANOUT = 5
CAP = 18
MAIN = 16
REST = CAP - MAIN
FRONT = 80
CHUNK = 112
GROUP = 16
VMEM_LIMIT = 28 * 1024 * 1024
BF = jnp.bfloat16
F32 = jnp.float32
I32 = jnp.int32
I16 = jnp.int16


def mm(a, b):
    return jnp.dot(a, b, preferred_element_type=F32)


def mm_nt(a, b):
    return lax.dot_general(a, b, (((1,), (1,)), ((), ())), preferred_element_type=F32)


def mm_tn(a, b):
    return lax.dot_general(a, b, (((0,), (0,)), ((), ())), preferred_element_type=F32)


def onehot(flag):
    return jnp.where(flag, jnp.ones((), BF), jnp.zeros((), BF))


def slot_kinds(me, slot, hots, ranks):
    t = slot.shape[1]
    row = lax.broadcasted_iota(I32, (32, t), 0)
    values = []
    for j, rank in enumerate(ranks):
        value = slot[j : j + 1, :]
        at = row == rank
        high = jnp.where(at, (value // 64).astype(F32), 0.0)
        low = jnp.where(at, (value % 64).astype(F32), 0.0)
        values.append(jnp.concatenate([high, low], axis=0).astype(BF))
    by_rank = mm_nt(jnp.concatenate(hots, axis=1), jnp.concatenate(values, axis=1)).astype(BF)
    source = lax.broadcasted_iota(I32, (64, 512), 0)
    target = lax.broadcasted_iota(I32, (64, 512), 1)
    rank, part = source % 32, source // 32
    in_main = rank < MAIN
    lane = jnp.where(in_main, (me % 8) * MAIN + rank, (me % 64) * REST + rank - MAIN)
    kind = jnp.where(in_main, 0, 2) + part
    return mm(by_rank, onehot((rank < CAP) & (target == kind * 128 + lane)))


def hub_sums(message, hub):
    rows = lax.broadcasted_iota(I16, (HUBS, message.shape[0]), 0)
    ids = hub[...].astype(I16)
    count = onehot(rows == ids[0:1, :]) + onehot(rows == ids[1:2, :])
    return mm(count, message[...]).astype(BF)


def half_sums(hubs, message, hub, h, a, g, out):
    depth = h.shape[1]

    @pl.when(hubs)
    def _():
        out[...] = hub_sums(message, hub)

    @pl.when(jnp.logical_not(hubs))
    def _():
        out[0:depth, :] = mm_tn(h[...], g[...]).astype(BF)
        out[depth : 2 * depth, :] = mm_tn(a[...], g[...]).astype(BF)


def find_places(chip_row, owner, slot, places, kinds):
    fan, t = slot.shape
    n = kinds.shape[0]
    device = lax.broadcasted_iota(I32, (n, t), 0)
    before = onehot(
        lax.broadcasted_iota(I16, (t, t), 0) < lax.broadcasted_iota(I16, (t, t), 1)
    )
    named = [device == owner[j] for j in range(fan)]
    hots = [onehot(f) for f in named]
    hot = jnp.concatenate(hots, axis=0)
    earlier = mm(hot, before)
    amount = jnp.sum(hot.astype(F32), axis=1, keepdims=True)
    base = jnp.zeros((n, 1), F32)
    ranks = []
    for j in range(fan):
        rank = jnp.where(named[j], earlier[j * n : (j + 1) * n, :] + base, 0.0)
        ranks.append(jnp.sum(rank, axis=0, keepdims=True).astype(I32))
        base = base + amount[j * n : (j + 1) * n, :]
    for j, rank in enumerate(ranks):
        in_main = rank < MAIN
        places[j : j + 1, :] = jnp.where(in_main, owner[j] * MAIN + rank, -1)
        places[4 + j : 5 + j, :] = jnp.where(in_main, -1, owner[j] * REST + (rank - MAIN))
    kinds[...] = slot_kinds(chip_row, slot[...], hots, ranks).astype(BF)


def grads_kernel(
    me, h_in, a_in, go_in, ws_in, wn_in, hub_in, owner_in, slot_in,
    h, a, g, hub, message, send, places, kinds,
    go, ws, wn, owner, slot, arrived,
):
    loads = [
        pltpu.make_async_copy(src, dst, arrived.at[i])
        for i, (src, dst) in enumerate(
            (
                (owner_in, owner), (slot_in, slot),
                (h_in, h), (ws_in, ws), (a_in, a), (wn_in, wn), (go_in, go), (hub_in, hub),
            )
        )
    ]
    for load in loads:
        load.start()

    loads[0].wait()
    loads[1].wait()
    find_places(me[0], owner, slot, places, kinds)
    loads[2].wait()
    loads[3].wait()
    pre = mm(h[...], ws[...])
    loads[4].wait()
    loads[5].wait()
    pre = pre + mm(a[...], wn[...])
    loads[6].wait()
    sig = jax.nn.sigmoid(pre)
    g[...] = (go[...].astype(F32) * (sig * (1.0 + pre * (1.0 - sig)))).astype(BF)
    message[...] = (mm_nt(g[...], wn[...]) * (1.0 / FANOUT)).astype(BF)
    loads[7].wait()
    half_sums(lax.rem(me[0], 2) == 1, message, hub, h, a, g, send)


def spread_rows():
    row = lax.broadcasted_iota(I32, (GROUP * 16, 192), 0)
    col = lax.broadcasted_iota(I32, (GROUP * 16, 192), 1)
    chunk, s = row // 16, row % 16
    want = jnp.where(s < 8, (s // 2) * 32 + chunk * 2 + s % 2, 128 + (s - 8) * 16 + chunk)
    return onehot((s < 12) & (col == want))


def picks(places, at):
    return onehot((at == places[0]) | (at == places[1]) | (at == places[2]))


def pack_kernel(me, h, a, g, hub, message, places, kinds, out, mine, g_out, stored):
    store = pltpu.make_async_copy(g, g_out, stored)
    store.start()
    t = message.shape[0]
    n = out.shape[0]
    half_sums(lax.rem(me[0], 2) == 0, message, hub, h, a, g, mine)
    main = [places[j : j + 1, :].astype(I16) for j in range(3)]
    last = [places[4 + j : 5 + j, :].astype(I16) for j in range(3)]
    msg = message[...]
    spread = spread_rows()
    rest = mm(picks(last, lax.broadcasted_iota(I16, (n * REST, t), 0)), msg).astype(BF)
    stacked = jnp.concatenate(
        [
            jnp.concatenate(
                [rest[k * 32 : (k + 1) * 32, q * 128 : (q + 1) * 128] for q in range(4)]
                + [kinds[k * GROUP : (k + 1) * GROUP, q * 128 : (q + 1) * 128] for q in range(4)],
                axis=0,
            )
            for k in range(n // GROUP)
        ],
        axis=1,
    )
    tiles = mm(spread, stacked).astype(BF)
    for k in range(n // GROUP):
        out[k * GROUP : (k + 1) * GROUP, 64:80, :] = tiles[:, k * 128 : (k + 1) * 128].reshape(
            GROUP, 16, 128
        )
    rows = mm(picks(main, lax.broadcasted_iota(I16, (n * MAIN, t), 0)), msg).astype(BF)
    for q in range(4):
        out[:, q * 16 : (q + 1) * 16, :] = rows[:, q * 128 : (q + 1) * 128].reshape(n, 16, 128)
    store.wait()


def join_kernel(mine, got, held, out):
    for half in range(2):
        for q in range(2):
            at = half * 256 + q * 128
            total = mine[:, at : at + 128].astype(F32) + got[:, at : at + 128].astype(F32)
            first = FRONT + q * 16
            out[:, half, first : first + 16, :] = total.astype(BF).reshape(-1, 16, 128)


def reduce_kernel(received, out, kept, total, left):
    chips, each = received.shape[0], total.shape[0]
    rows = pltpu.make_async_copy(received.at[:, :, pl.ds(0, FRONT), :], kept, left.at[0])
    rows.start()
    acc = jnp.sum(received[:, :, FRONT : FRONT + 32, :].astype(F32), axis=0, keepdims=True)
    total[...] = jnp.broadcast_to(acc.astype(BF), total.shape)
    copies = [
        pltpu.make_async_copy(total, out.at[pl.ds(i * each, each)], left.at[1 + i])
        for i in range(chips // each)
    ]
    for copy in copies:
        copy.start()
    for copy in copies:
        copy.wait()
    rows.wait()


def front_kernel(received, g, ws, out, grad_self, rows, index):
    step = pl.program_id(0)
    n = received.shape[0]
    grad_self[...] = mm_nt(g[...], ws[...]).astype(BF)

    @pl.when(step == 0)
    def _():
        for q in range(4):
            rows[0 : n * MAIN, q * 128 : (q + 1) * 128] = received[
                :, q * 16 : (q + 1) * 16, :
            ].reshape(n * MAIN, 128)
        spread = spread_rows()
        main = []
        rest = [jnp.zeros((1, 128), F32), jnp.zeros((1, 128), F32)]
        for k in range(n // GROUP):
            tile = received[k * GROUP : (k + 1) * GROUP, 64:80, :].reshape(GROUP * 16, 128)
            stacked = mm_tn(spread, tile)
            for q in range(4):
                rows[n * MAIN + k * 32 : n * MAIN + (k + 1) * 32, q * 128 : (q + 1) * 128] = (
                    stacked[q * 32 : (q + 1) * 32, :].astype(BF)
                )
            main_slot = stacked[128:144, :] * 64.0 + stacked[144:160, :]
            rest_slot = stacked[160:176, :] * 64.0 + stacked[176:192, :]
            main.append(jnp.sum(main_slot[0:8, :], axis=0, keepdims=True))
            main.append(jnp.sum(main_slot[8:16, :], axis=0, keepdims=True))
            part = k * GROUP // 64
            rest[part] = rest[part] + jnp.sum(rest_slot, axis=0, keepdims=True)
        for g, line in enumerate(main + rest):
            index[g : g + 1, :] = line.astype(I32)

    block = out.shape[0]
    wanted = lax.broadcasted_iota(I32, (block, 128), 0) + step * block
    hot = jnp.concatenate(
        [onehot(wanted == index[g : g + 1, :]) for g in range(n * CAP // 128)], axis=1
    )
    out[...] = mm(hot, rows[...])


def fill_kernel(scale, mine, me, part, *refs):
    hub_grad, grad_w_self, grad_w_neigh, wide, done = refs[-5:]
    depth = grad_w_self.shape[0]
    hubs = (lax.rem(me[0], 2) == 0) == mine
    factor = jnp.where(hubs, 1.0, scale)
    steps = 4
    rows = HUBS // steps
    chips = rows // 16

    def copies(step):
        src = wide.at[pl.ds(step * rows, rows)]
        to_hubs = hub_grad.at[pl.ds(step * rows, rows)]
        weights = grad_w_self if step < steps // 2 else grad_w_neigh
        to_weights = weights.at[pl.ds(step * rows % depth, rows)]
        return (
            pltpu.make_async_copy(src, to_hubs, done.at[step]),
            pltpu.make_async_copy(src, to_weights, done.at[step]),
        )

    for step in range(steps):
        for half in range(2):
            for q in range(2):
                at = half * 256 + q * 128
                block = part[step * chips : (step + 1) * chips, half, q * 16 : (q + 1) * 16, :]
                wide[step * rows : (step + 1) * rows, at : at + 128] = (
                    block.reshape(rows, 128).astype(F32) * factor
                )
        to_hubs, to_weights = copies(step)
        pl.when(hubs)(to_hubs.start)
        pl.when(jnp.logical_not(hubs))(to_weights.start)
    for step in range(steps):
        to_hubs, to_weights = copies(step)
        pl.when(hubs)(to_hubs.wait)
        pl.when(jnp.logical_not(hubs))(to_weights.wait)


SMEM = pl.BlockSpec(memory_space=pltpu.SMEM)
HBM = pl.BlockSpec(memory_space=pltpu.HBM)
VMEM = pl.BlockSpec(memory_space=pltpu.VMEM)
PARAMS = pltpu.CompilerParams(vmem_limit_bytes=VMEM_LIMIT)


def in_hbm(x):
    return pltpu.with_memory_space_constraint(x, pltpu.HBM)


def in_vmem(x):
    return pltpu.with_memory_space_constraint(x, pltpu.VMEM)


def body(h_self, agg, grad_out, w_self, w_neigh, owner, slot, hub_refs):
    t, width = h_self.shape
    n = lax.axis_size("dev")
    me = lax.axis_index("dev").astype(I32).reshape(1)
    owner_t = owner.transpose(1, 2, 0)
    slot_t = slot.T
    hub_t = hub_refs.T
    swap = [(i, i ^ 1) for i in range(n)]

    with jax.named_scope("grads"):
        h, a, g, hub, message, send, places, kinds = pl.pallas_call(
            grads_kernel,
            out_shape=(
                pltpu.VMEM((t, width), BF),
                pltpu.VMEM((t, width), BF),
                pltpu.VMEM((t, width), BF),
                pltpu.VMEM(hub_t.shape, I32),
                pltpu.VMEM((t, width), BF),
                pltpu.VMEM((HUBS, width), BF),
                pltpu.VMEM((8, t), I32),
                pltpu.VMEM((n, 512), BF),
            ),
            in_specs=[SMEM] + [HBM] * 8,
            out_specs=[VMEM] * 8,
            scratch_shapes=[
                pltpu.VMEM((t, width), BF),
                pltpu.VMEM((width, width), BF),
                pltpu.VMEM((width, width), BF),
                pltpu.VMEM(owner_t.shape, I32),
                pltpu.VMEM(slot_t.shape, I32),
                pltpu.SemaphoreType.DMA((8,)),
            ],
            compiler_params=PARAMS,
        )(me, *map(in_hbm, (h_self, agg, grad_out, w_self, w_neigh, hub_t, owner_t, slot_t)))
    with jax.named_scope("core_exchange"):
        got = lax.ppermute(send, "dev", swap)
    with jax.named_scope("pack"):
        packed, mine, g_kept = pl.pallas_call(
            pack_kernel,
            out_shape=(
                pltpu.VMEM((n, CHUNK, 128), BF),
                pltpu.VMEM((HUBS, width), BF),
                pltpu.HBM((t, width), BF),
            ),
            in_specs=[SMEM] + [VMEM] * 7,
            out_specs=[VMEM] * 2 + [HBM],
            scratch_shapes=[pltpu.SemaphoreType.DMA],
            compiler_params=PARAMS,
        )(me, *map(in_vmem, (h, a, g, hub, message, places, kinds)))
    with jax.named_scope("join"):
        packed = pl.pallas_call(
            join_kernel,
            out_shape=pltpu.VMEM((n // 2, 2, CHUNK, 128), BF),
            in_specs=[VMEM, VMEM, HBM],
            out_specs=VMEM,
            input_output_aliases={2: 0},
            compiler_params=PARAMS,
        )(in_vmem(mine), in_vmem(got), in_vmem(packed.reshape(n // 2, 2, CHUNK, 128)))
    with jax.named_scope("rows_to_owners"):
        received = lax.all_to_all(
            packed.reshape(n, CHUNK, 128), "dev", split_axis=0, concat_axis=0, tiled=True
        )
    with jax.named_scope("sum_parts"):
        total, kept = pl.pallas_call(
            reduce_kernel,
            out_shape=(
                pltpu.HBM((n // 2, 2, 32, 128), BF),
                pltpu.HBM((n // 2, 2, FRONT, 128), BF),
            ),
            in_specs=[VMEM],
            out_specs=[HBM] * 2,
            scratch_shapes=[
                pltpu.VMEM((8, 2, 32, 128), BF),
                pltpu.SemaphoreType.DMA((1 + n // 16,)),
            ],
            compiler_params=PARAMS,
        )(in_vmem(received.reshape(n // 2, 2, CHUNK, 128)))
        kept = kept.reshape(n, FRONT, 128)
    with jax.named_scope("sums_to_all"):
        own = lax.all_to_all(
            total.reshape(n, 32, 128), "dev", split_axis=0, concat_axis=0, tiled=True
        )
    with jax.named_scope("front"):
        front_grad, grad_self = pl.pallas_call(
            front_kernel,
            out_shape=(
                jax.ShapeDtypeStruct((OWN_DEV, width), F32),
                jax.ShapeDtypeStruct((t, width), BF),
            ),
            grid=(8,),
            in_specs=[
                pl.BlockSpec((n, FRONT, 128), lambda i: (0, 0, 0)),
                pl.BlockSpec((t // 8, width), lambda i: (i, 0)),
                pl.BlockSpec((width, width), lambda i: (0, 0)),
            ],
            out_specs=(
                pl.BlockSpec((OWN_DEV // 8, width), lambda i: (i, 0)),
                pl.BlockSpec((t // 8, width), lambda i: (i, 0)),
            ),
            scratch_shapes=[
                pltpu.VMEM((n * CAP, width), BF),
                pltpu.VMEM((24, 128), I32),
            ],
            compiler_params=PARAMS,
            cost_estimate=pl.CostEstimate(
                flops=2 * OWN_DEV * n * CAP * width, bytes_accessed=8 << 20, transcendentals=0
            ),
        )(in_hbm(kept), in_hbm(g_kept), in_hbm(w_self))
    own, front_grad = lax.optimization_barrier((own, front_grad))
    with jax.named_scope("core_exchange_back"):
        other = lax.ppermute(own, "dev", swap)
    scale = 1.0 / (t * n) ** 0.5
    filled = ()
    for mine_too, part in ((True, own), (False, other)):
        with jax.named_scope("fill_own" if mine_too else "fill_other"):
            filled = pl.pallas_call(
                functools.partial(fill_kernel, scale, mine_too),
                out_shape=(
                    jax.ShapeDtypeStruct((HUBS, width), F32),
                    jax.ShapeDtypeStruct((width, width), F32),
                    jax.ShapeDtypeStruct((width, width), F32),
                ),
                in_specs=[SMEM, VMEM] + [HBM] * len(filled),
                out_specs=[HBM] * 3,
                scratch_shapes=[pltpu.VMEM((HUBS, width), F32), pltpu.SemaphoreType.DMA((4,))],
                input_output_aliases={2 + i: i for i in range(len(filled))},
                compiler_params=PARAMS,
                cost_estimate=pl.CostEstimate(
                    flops=HUBS * width, bytes_accessed=3 << 20, transcendentals=0
                ),
            )(me, part.reshape(n // 2, 2, 32, 128), *filled)
    hub_grad, grad_w_self, grad_w_neigh = filled
    return grad_self, front_grad, hub_grad, grad_w_self, grad_w_neigh


def solution(mesh):
    placed = (
        P("dev", None),
        P("dev", None),
        P("dev", None),
        P(),
        P(),
        P("dev", None, None),
        P("dev", None),
        P("dev", None),
    )
    return jax.shard_map(
        body,
        mesh=mesh,
        in_specs=placed,
        out_specs=(P("dev", None), P("dev", None), P(), P(), P()),
        check_vma=False,
    )
```
